512 devices in a mesh: row: 16 (over z), col: 32 (over y, x, core).
Axes of the slice: x: 4, y: 4, z: 16, core: 2. Of those that a mesh axis runs over, the one named last changes fastest.
Arguments:
- positions: float32 [3, 524288], P(None, ('row', 'col')), may hold values from -5 to 5
- velocities: float32 [3, 524288], P(None, ('row', 'col')), may hold values from -3 to 3
- accels: float32 [3, 524288], P(None, ('row', 'col')), may hold values from -3 to 3
- jerks: float32 [3, 524288], P(None, ('row', 'col')), may hold values from -24 to 24
- masses: float32 [1, 524288], P(None, ('row', 'col')), may hold values from 0.25 to 4
- elapsed: float32 [1, 524288], P(None, ('row', 'col')), may hold values from 0.0625 to 0.5
- active: int32 [32768], P('row'), may hold values from 0 to 524287, as said below
- live_tiles: int32 [16], P('row'), may hold values from 1 to 16, as said below
Outputs:
- new_positions: float32 [3, 524288], P(None, ('row', 'col'))
- new_velocities: float32 [3, 524288], P(None, ('row', 'col'))
- new_accels: float32 [3, 524288], P(None, ('row', 'col'))
- new_jerks: float32 [3, 524288], P(None, ('row', 'col'))
The draws below stay inside these ranges and needn't reach their ends.
Inputs may be any that keep to these rules, and one draw needn't show every extreme that they name: `active`: all 32768 entries are different star indices, live and not. `live_tiles`: some index of row has all its tiles live in every draw.
All inputs are finite; a program needn't handle non-finite values.
Results may differ from the reference program's by a relative error of at most 0.0001.
Values sent between devices are 32-bit elements; how exact they have to be, the bound alone decides.
A program may use at most 128 MiB of HBM per device.

```python
import math
import jax
import jax.numpy as jnp
from jax import lax

JS = 16384
ACT_ROW = 2048
TILE = 128
NSTARS = 524288
ACTIVE = 32768
N_ROW = 16
N_COL = 32


def common_lists(key):
    capt = ACT_ROW // TILE
    k_one, k_two, k_three, k_four = jax.random.split(key, 4)
    first = jax.random.randint(k_one, (N_ROW,), 0, capt)
    second = jax.random.randint(k_two, (N_ROW,), 0, capt)
    counts = 1 + first * second // capt
    fullest = jax.random.randint(k_three, (), 0, N_ROW)
    counts = jnp.where(jnp.arange(N_ROW) == fullest, capt, counts)
    stars = jax.random.permutation(k_four, NSTARS)[:ACTIVE]
    return (stars.astype(jnp.int32), counts.astype(jnp.int32))


def draw_active(key, part):
    stars, counts = common_lists(key)
    return stars


def draw_live_tiles(key, part):
    stars, counts = common_lists(key)
    return counts


def levels(own_key, shape, cuts, smallest, high):
    level, own = 1.0, jax.random.fold_in(own_key, 6)
    for position, parts in cuts:
        draws = jnp.exp(jax.random.uniform(jax.random.fold_in(own, position), (parts,), jnp.float32, smallest / len(cuts), high / len(cuts)))
        level = level * jnp.repeat(draws, shape[position] // parts).reshape([-1 if axis == position else 1 for axis in range(len(shape))])
    return level


def gaussian(key, extent, deviation, bound, cuts=(), held_as=jnp.bfloat16):
    factor_of = levels(key, extent, cuts, -0.22, 0.18) if cuts else 1.0
    result = jax.random.normal(key, extent, jnp.float32) * deviation * factor_of
    return jnp.minimum(jnp.maximum(result, -bound), bound).astype(held_as)


def setup_inputs(seed: int = 0) -> dict:
    keys = jax.random.split(jax.random.key(seed), 9)
    return {
        "positions": gaussian(keys[0], (3, NSTARS), 1.0, 5.0, ((1, 512),), jnp.float32),
        "velocities": gaussian(keys[1], (3, NSTARS), 0.5, 3.0, ((1, 512),), jnp.float32),
        "accels": gaussian(keys[2], (3, NSTARS), 0.5, 3.0, ((1, 512),), jnp.float32),
        "jerks": gaussian(keys[3], (3, NSTARS), 4.0, 24.0, ((1, 512),), jnp.float32),
        "masses": jnp.clip(jnp.exp(math.log(4.0) - 2.7725887 * jax.random.uniform(keys[4], (1, NSTARS), jnp.float32) ** levels(keys[4], (1, NSTARS), ((1, 512),), -0.2, 0.2)), 0.25, 4.0),
        "elapsed": jnp.clip(jnp.exp(math.log(0.5) - 2.0794415 * jax.random.uniform(keys[5], (1, NSTARS), jnp.float32) ** levels(keys[5], (1, NSTARS), ((1, 512),), -0.2, 0.2)), 0.0625, 0.5),
        "active": draw_active(jax.random.fold_in(keys[8], 71), 0),
        "live_tiles": draw_live_tiles(jax.random.fold_in(keys[8], 71), 0),
    }


EPS2 = 0.01

def predict(pos, vel, acc, jerk, step):
    x_pred = pos + step * (vel + step * (0.5 * acc + step * jerk / 6.0))
    v_pred = vel + step * (acc + step * (0.5 * jerk))
    return (x_pred, v_pred)

def pair_sums(i_pos, i_vel, j_pos, j_vel, j_weight):
    dx = j_pos[:, None, :] - i_pos[:, :, None]
    dv = j_vel[:, None, :] - i_vel[:, :, None]
    r_two = lax.optimization_barrier(jnp.sum(dx * dx, axis=0)) + EPS2
    inv_two = 1.0 / r_two
    scale = j_weight * jnp.sqrt(inv_two) * inv_two
    radial = 3.0 * lax.optimization_barrier(jnp.sum(dx * dv, axis=0)) * inv_two
    accel = lax.optimization_barrier(jnp.sum(scale * dx, axis=2))
    jerk = lax.optimization_barrier(jnp.sum(scale * (dv - radial * dx), axis=2))
    return jnp.concatenate([accel, jerk], 0)

def correct(pos, vel, acc, jerk, step, new_acc, new_jerk):
    v_new = vel + 0.5 * step * (acc + new_acc) + step * step / 12.0 * (jerk - new_jerk)
    x_new = pos + 0.5 * step * (vel + v_new) + step * step / 12.0 * (acc - new_acc)
    return (x_new, v_new)

def reference(positions, velocities, accels, jerks, masses, elapsed, active, live_tiles):
    weight = masses / NSTARS
    x_pred, v_pred = predict(positions, velocities, accels, jerks, elapsed)
    per_row = ACT_ROW // TILE
    slot = jnp.arange(ACTIVE)
    live = slot % ACT_ROW // TILE < live_tiles[slot // ACT_ROW]
    safe = active
    state = jnp.concatenate([jnp.take(x_pred, safe, axis=1), jnp.take(v_pred, safe, axis=1)], 0)
    ntile = ACTIVE // TILE
    i_tiles = state.reshape(6, ntile, TILE).transpose(1, 0, 2)
    jpb = x_pred.reshape(3, N_COL, JS).transpose(1, 0, 2)
    jvb = v_pred.reshape(3, N_COL, JS).transpose(1, 0, 2)
    jwb = weight.reshape(1, N_COL, JS).transpose(1, 0, 2)

    def one_tile(tile_state):

        def add_block(carry, blk):
            return (carry + pair_sums(tile_state[0:3], tile_state[3:6], blk[0], blk[1], blk[2]), None)
        out, _ = lax.scan(add_block, jnp.zeros((6, TILE), jnp.float32), (jpb, jvb, jwb))
        return out
    forces = lax.map(one_tile, i_tiles).transpose(1, 0, 2).reshape(6, ACTIVE)
    target = jnp.where(live, active, NSTARS).astype(jnp.int32)
    new_both = jnp.zeros((6, NSTARS), jnp.float32).at[:, target].set(forces, mode='drop')
    flag = jnp.zeros((1, NSTARS), jnp.float32).at[:, target].set(jnp.ones((1, ACTIVE), jnp.float32), mode='drop')
    is_on = flag > 0.5
    new_acc = new_both[0:3]
    new_jerk = new_both[3:6]
    x_new, v_new = correct(positions, velocities, accels, jerks, elapsed, new_acc, new_jerk)
    return (jnp.where(is_on, x_new, positions), jnp.where(is_on, v_new, velocities), jnp.where(is_on, new_acc, accels), jnp.where(is_on, new_jerk, jerks))
```

```python
import functools

import jax
import jax.numpy as jnp
from jax import lax
from jax.experimental import pallas as pl
from jax.experimental.pallas import tpu as pltpu
from jax.sharding import PartitionSpec as P

TILE = 128
EPS2 = 0.01
LANES = 128
BLOCK_J = 2048
PIECE_J = 512
PARTS = 16
MESH = pl.DeviceIdType.MESH
VMEM = pltpu.VMEM
F32 = jnp.float32
BF16 = jnp.bfloat16


def vmem():
    return pl.BlockSpec(memory_space=pltpu.VMEM)


def smem():
    return pl.BlockSpec(memory_space=pltpu.SMEM)


def split3(x):
    high = x.astype(BF16).astype(F32)
    rest = x - high
    mid = rest.astype(BF16).astype(F32)
    return high, mid, rest - mid


class Place:
    def __init__(self, rows, cols):
        self.rows, self.cols = rows, cols
        self.side = {32: 4, 8: 2}[cols]
        self.half = self.side // 2
        self.cubes = rows // 2 * self.half * self.half
        self.row = lax.axis_index("row")
        self.col = lax.axis_index("col")
        self.y = self.col // (2 * self.side)
        self.x = lax.rem(self.col // 2, self.side)
        self.core = lax.rem(self.col, 2)
        self.cube = (self.row // 2 * self.half + self.y // 2) * self.half + self.x // 2
        self.member = self.member_at(self.row)

    def member_at(self, row):
        return ((lax.rem(row, 2) * 2 + lax.rem(self.y, 2)) * 2 + lax.rem(self.x, 2)) * 2 + self.core

    def device(self, row, y, x, core):
        return {"row": row, "col": (y * self.side + x) * 2 + core}

    def in_cube(self, member):
        return self.device(
            self.row // 2 * 2 + member // 8,
            self.y // 2 * 2 + lax.rem(member // 4, 2),
            self.x // 2 * 2 + lax.rem(member // 2, 2),
            lax.rem(member, 2),
        )

    def in_other(self, cube):
        return self.device(
            cube // (self.half * self.half) * 2 + lax.rem(self.row, 2),
            lax.rem(cube // self.half, self.half) * 2 + lax.rem(self.y, 2),
            lax.rem(cube, self.half) * 2 + lax.rem(self.x, 2),
            self.core,
        )


def signal(device):
    pl.semaphore_signal(pltpu.get_barrier_semaphore(), inc=1, device_id=device, device_id_type=MESH)


def await_greetings(count):
    pl.semaphore_wait(pltpu.get_barrier_semaphore(), count)


def each(first, last, body, step=1):
    def one(n, carry):
        body(first + n * step)
        return carry

    lax.fori_loop(0, (last - first + step - 1) // step, one, 0)


def remote(source, target, send, recv, device):
    return pltpu.make_async_remote_copy(
        src_ref=source, dst_ref=target, send_sem=send, recv_sem=recv, device_id=device, device_id_type=MESH
    )


def await_bytes(ref, semaphore):
    pltpu.make_async_copy(ref, ref, semaphore).wait()


def gather_kernel(rows, cols, total_stars, pos, vel, acc, jerk, mass, step, msg, shard, ids, id_send, id_recv, send, recv):
    at = Place(rows, cols)
    me = at.member
    each(1, PARTS, lambda d: signal(at.in_cube(lax.rem(me + d, PARTS))))
    each(1, rows, lambda d: signal({"row": lax.rem(at.row + d, rows)}))
    dt = step[...]
    a, j, v = acc[...], jerk[...], vel[...]
    shard[me, 0:3, :] = pos[...] + dt * (v + dt * (0.5 * a + dt * j / 6.0))
    shard[me, 3:4, :] = mass[...] / total_stars
    shard[me, 4:7, :] = v + dt * (a + dt * (0.5 * j))
    shard[me, 7:8, :] = jnp.ones_like(dt)
    ids[at.row] = msg[me]
    await_greetings(PARTS + rows - 2)

    def send_ids(d):
        peer = lax.rem(at.row + d, rows)
        remote(msg.at[at.member_at(peer)], ids.at[at.row], id_send, id_recv, {"row": peer}).start()

    def send_block(d):
        peer = lax.rem(me + d, PARTS)
        remote(shard.at[me], shard.at[me], send, recv, at.in_cube(peer)).start()

    each(1, rows, send_ids)
    each(1, PARTS, send_block)
    await_bytes(ids.at[pl.ds(0, rows - 1)], id_recv)
    await_bytes(ids.at[pl.ds(0, rows - 1)], id_send)
    await_bytes(shard.at[pl.ds(0, PARTS - 1)], recv)
    await_bytes(shard.at[pl.ds(0, PARTS - 1)], send)


def pick_kernel(rows, cols, width, counts, shard, ids, out, packed, table):
    at = Place(rows, cols)
    chunks = width // LANES
    high_count = PARTS * chunks
    features = (0, 1, 2, 4, 5, 6)
    groups = 4
    for order, f in enumerate(features):
        plane = jnp.concatenate([shard[:, f, c * LANES : (c + 1) * LANES] for c in range(chunks)], 0)
        h, m, l = split3(plane)
        table[order * high_count : (order + 1) * high_count, :] = jnp.concatenate([h, m, l], 1).astype(BF16)

    packed[...] = jnp.full(packed.shape, -1, jnp.int32)
    lane = lax.broadcasted_iota(jnp.int32, (8, LANES), 1)

    def pack(q, offset):
        t, shift = offset // LANES, lax.rem(offset, LANES)
        rolled = pltpu.roll(jnp.broadcast_to(ids[q, 0:1, :], (8, LANES)), shift, 1)
        packed[t] = jnp.where(lane >= shift, rolled, packed[t])
        packed[t + 1] = jnp.where(lane < shift, rolled, packed[t + 1])
        return offset + counts[q, 1, 0] * (TILE // PARTS)

    used = lax.fori_loop(0, rows, pack, 0)

    def part(g, carry):
        first = g * groups
        star = jnp.concatenate([packed[first + n, 0:1, :] for n in range(groups)], 1)
        owner = star // width
        row, col = owner // cols, lax.rem(owner, cols)
        y, x = col // (2 * at.side), lax.rem(col // 2, at.side)
        cube = (row // 2 * at.half + y // 2) * at.half + x // 2
        member = ((lax.rem(row, 2) * 2 + lax.rem(y, 2)) * 2 + lax.rem(x, 2)) * 2 + lax.rem(col, 2)
        mine = (star >= 0) & (cube == at.cube)
        place = lax.rem(star, width)
        high = jnp.where(mine, place // LANES * PARTS + member, -1)
        low = lax.rem(place, LANES)
        span = groups * LANES
        pick = jnp.where(lax.broadcasted_iota(jnp.int32, (LANES, span), 0) == low, 1.0, 0.0).astype(BF16)
        pick = jnp.concatenate([pick, pick, pick], 0)
        at_row = lax.broadcasted_iota(jnp.int32, (high_count, span), 0) == high
        for order, f in enumerate(features):
            values = jnp.dot(table[order * high_count : (order + 1) * high_count, :], pick, preferred_element_type=F32)
            found = jnp.sum(jnp.where(at_row, values, 0.0), axis=0, keepdims=True)
            for n in range(groups):
                out[2 * (first + n) + f // 4, f % 4 : f % 4 + 1, :] = found[:, n * LANES : (n + 1) * LANES]
        return carry

    out[...] = jnp.zeros_like(out)
    lax.fori_loop(0, (used + groups * LANES - 1) // (groups * LANES), part, 0)


def cube_sum_kernel(rows, cols, blocks, out, arrived, send_a, recv_a, send_b, recv_b):
    at = Place(rows, cols)
    me, cubes = at.cube, at.cubes
    share = blocks.shape[0] // cubes
    peer_of = lambda d: lax.rem(me + d, cubes)
    each(1, cubes, lambda d: signal(at.in_other(peer_of(d))))
    mine = pl.ds(me * share, share)
    arrived[me] = blocks[mine]
    await_greetings(cubes - 1)

    def scatter(d):
        peer = peer_of(d)
        remote(blocks.at[pl.ds(peer * share, share)], arrived.at[me], send_a, recv_a, at.in_other(peer)).start()

    each(1, cubes, scatter)
    await_bytes(arrived.at[pl.ds(0, cubes - 1)], recv_a)
    out[mine] = jnp.sum(arrived[...], axis=0)
    each(1, cubes, lambda d: remote(out.at[mine], out.at[mine], send_b, recv_b, at.in_other(peer_of(d))).start())
    await_bytes(out.at[pl.ds(0, (cubes - 1) * share)], recv_b)
    await_bytes(arrived.at[pl.ds(0, cubes - 1)], send_a)
    await_bytes(out.at[pl.ds(0, (cubes - 1) * share)], send_b)


def sweep_kernel(rows, cols, counts, shard, packed, states, out, j_side, j_mass):
    at = Place(rows, cols)
    width = shard.shape[2]
    total = PARTS * width
    row_of = lambda shape: lax.broadcasted_iota(jnp.int32, shape, 0)
    at8 = row_of((8, LANES))

    def dots(tile):
        first = row_of(tile.shape) < 3
        swapped = pltpu.roll(tile, 4, 0)
        norm = jnp.sum(jnp.where(first, tile * tile, 0.0), axis=0, keepdims=True)
        cross = jnp.sum(jnp.where(first, tile * swapped, 0.0), axis=0, keepdims=True)
        return norm, cross

    def prepare(z, carry):
        tile = shard[z]
        norm, cross = dots(tile)
        h, m, l = split3(tile)
        pieces = split3(norm) + split3(cross)
        line = row_of(tile.shape)
        extra = jnp.zeros_like(tile)
        for n, piece in enumerate(pieces):
            extra = jnp.where(line == n, piece, extra)
        place = pl.ds(pl.multiple_of(z * width, width), width)
        j_side[:, place] = jnp.concatenate([h, h, h, m, m, l, extra, jnp.zeros_like(tile)], 0).astype(BF16)
        h, m, l = split3(tile * tile[3:4, :])
        j_mass[:, place] = jnp.concatenate([h, m, l, jnp.zeros_like(tile)], 0).astype(BF16)
        return carry

    lax.fori_loop(0, PARTS, prepare, 0)
    out[...] = jnp.zeros_like(out)

    def left_of(tile):
        norm, cross = dots(tile)
        h, m, l = split3(tile)
        nh, nm, nl = split3(norm + EPS2)
        ch, cm, cl = split3(cross)
        zero = jnp.zeros_like(tile)

        def for_r(piece, last):
            return jnp.where(at8 < 3, -2.0 * piece, jnp.where(at8 == 7, last, 0.0))

        def for_b(piece, last):
            return jnp.where(at8 == 7, last, jnp.where(at8 == 3, 0.0, -pltpu.roll(piece, 4, 0)))

        r_extra = jnp.where(at8 < 3, 1.0, 0.0)
        b_extra = jnp.where((at8 >= 3) & (at8 < 6), 1.0, 0.0)
        blank = jnp.zeros((64, LANES), F32)
        left_r = jnp.concatenate(
            [for_r(h, nh), for_r(m, nm), for_r(l, nl), for_r(h, 0.0), for_r(m, 0.0), for_r(h, 0.0), r_extra, zero, blank], 0
        )
        left_b = jnp.concatenate(
            [for_b(h, ch), for_b(m, cm), for_b(l, cl), for_b(h, 0.0), for_b(m, 0.0), for_b(h, 0.0), b_extra, zero, blank], 0
        )
        return left_r.T[:, 0:64], left_b.T[:, 0:64]

    def run(t, count):
        span = count * LANES
        tiles = [jnp.concatenate([states[2 * (t + n)], states[2 * (t + n) + 1]], 0) for n in range(count)]
        lefts = [left_of(tile) for tile in tiles]
        left = jnp.concatenate([l[0] for l in lefts] + [l[1] for l in lefts], 0).astype(BF16)

        def one_block(n, sums):
            def place(s):
                return pl.ds(pl.multiple_of(n * BLOCK_J + s * PIECE_J, PIECE_J), PIECE_J)

            def distances(s):
                return jnp.dot(left, j_side[:, place(s)], preferred_element_type=F32)

            ahead = distances(0)
            for s in range(BLOCK_J // PIECE_J):
                both = ahead
                if s + 1 < BLOCK_J // PIECE_J:
                    ahead = distances(s + 1)
                inverse = lax.rsqrt(both[0:span])
                square = inverse * inverse
                near = square * inverse
                tilt = near * square * both[span:]
                pair = jnp.concatenate([near, tilt], 0)
                high = pair.astype(BF16)
                low = (pair - high.astype(F32)).astype(BF16)
                weights = j_mass[:, place(s)]
                sums += lax.dot_general(
                    jnp.concatenate([high, low], 1),
                    jnp.concatenate([weights, weights], 1),
                    (((1,), (1,)), ((), ())),
                    preferred_element_type=F32,
                )
            return sums

        sums = lax.fori_loop(0, total // BLOCK_J, one_block, jnp.zeros((2 * span, 32), F32))
        sums = jnp.concatenate([sums, jnp.zeros((2 * span, LANES - 32), F32)], 1)
        for n, tile in enumerate(tiles):
            near = sums[n * LANES : (n + 1) * LANES].T
            tilt = sums[span + n * LANES : span + (n + 1) * LANES].T
            near = near[0:8] + near[8:16] + near[16:24]
            tilt = tilt[0:8] + tilt[8:16] + tilt[16:24]
            near = near - tile * near[7:8]
            tilt = tilt - tile * tilt[7:8]
            force = near - jnp.where(at8 >= 4, 3.0 * pltpu.roll(tilt, 4, 0), 0.0)
            star = packed[t + n]
            force = jnp.where(star >= 0, force, 0.0)
            force = jnp.where(at8 == 3, jnp.where(at.cube == 0, star.astype(F32), 0.0), force)
            out[2 * (t + n)] = force[0:4]
            out[2 * (t + n) + 1] = force[4:8]

    live = lax.fori_loop(0, rows, lambda q, n: n + counts[q, 1, 0], 0)
    tiles = (live + PARTS - 1) // PARTS

    def two(n, carry):
        run(2 * n, 2)
        return carry

    lax.fori_loop(0, tiles // 2, two, 0)

    @pl.when(lax.rem(tiles, 2) == 1)
    def _():
        run(tiles - 1, 1)


def deliver_kernel(rows, cols, blocks, out, arrived, lined, sends, recvs):
    at = Place(rows, cols)
    me, cubes, side = at.cube, at.cubes, at.side
    share = blocks.shape[0] // cubes
    plane = side * side
    here = at.y * side + at.x
    peer_of = lambda d: lax.rem(me + d, cubes)
    sibling = at.device(at.row, at.y, at.x, 1 - at.core)

    def beside(d):
        spot = lax.rem(here + d, plane)
        return at.device(at.row, spot // side, lax.rem(spot, side), at.core)

    each(1, cubes, lambda d: signal(at.in_other(peer_of(d))))
    each(1, rows, lambda d: signal({"row": lax.rem(at.row + d, rows)}))
    each(1, plane, lambda d: signal(beside(d)))
    signal(sibling)
    arrived[me] = blocks[pl.ds(me * share, share)]
    await_greetings(cubes + rows + plane - 2)

    def scatter(d):
        peer = peer_of(d)
        part = blocks.at[pl.ds(peer * share, share)]
        remote(part, arrived.at[me], sends.at[0], recvs.at[0], at.in_other(peer)).start()

    each(1, cubes, scatter)
    others = arrived.at[pl.ds(0, cubes - 1)]
    await_bytes(others, recvs.at[0])
    lined[at.row] = jnp.sum(arrived[...], axis=0)

    def along(d):
        mine = lined.at[at.row]
        remote(mine, mine, sends.at[1], recvs.at[1], {"row": lax.rem(at.row + d, rows)}).start()

    each(1, rows, along)
    line = lined.at[pl.ds(0, rows - 1)]
    await_bytes(line, recvs.at[1])

    each(1, plane, lambda d: remote(lined, out.at[at.core, here], sends.at[2], recvs.at[2], beside(d)).start())
    remote(lined, out.at[at.core, here], sends.at[3], recvs.at[3], sibling).start()
    out[at.core, here] = lined[...]
    await_bytes(out.at[0, pl.ds(0, plane - 1)], recvs.at[2])

    def forward(d):
        block = out.at[at.core, lax.rem(here + d, plane)]
        remote(block, block, sends.at[3], recvs.at[3], sibling).start()

    each(1, plane, forward)
    await_bytes(out.at[0], recvs.at[3])
    await_bytes(others, sends.at[0])
    await_bytes(line, sends.at[1])
    await_bytes(out.at[0, pl.ds(0, plane - 1)], sends.at[2])
    await_bytes(out.at[0], sends.at[3])


def finish_kernel(
    rows, cols, counts, forces, pos, vel, acc, jerk, step, new_pos, new_vel, new_acc, new_jerk, total, lined
):
    at = Place(rows, cols)
    width = pos.shape[1]
    highs = width // LANES
    mine = at.row * cols + at.col
    features = (0, 1, 2, 4, 5, 6)
    share = forces.shape[3]
    together = 8
    at8 = lax.broadcasted_iota(jnp.int32, (highs, LANES), 0)
    at_low = lax.broadcasted_iota(jnp.int32, (LANES, LANES), 0)
    total[...] = jnp.zeros_like(total)

    def one(n, carry):
        t, first = n // (PARTS // together), lax.rem(n, PARTS // together) * together
        lefts, rights = [], []
        for k in range(together):
            member = first + k
            spots = []
            for b in range(2):
                cube = (2 * t + b) // share
                z = cube // (at.half * at.half) * 2 + member // 8
                y = lax.rem(cube // at.half, at.half) * 2 + lax.rem(member // 4, 2)
                x = lax.rem(cube, at.half) * 2 + lax.rem(member // 2, 2)
                spots.append((lax.rem(member, 2), y * at.side + x, z, lax.rem(2 * t + b, share)))
            star = forces[(*spots[0], slice(3, 4), slice(None))].astype(jnp.int32)
            ok = (star >= 0) & (star // width == mine)
            place = lax.rem(star, width)
            here = jnp.where(ok, place // LANES, -1) == at8
            low = lax.rem(place, LANES)
            rights.append(jnp.where(at_low == low, 1.0, 0.0).astype(BF16))
            pieces = [[], [], []]
            for f in features:
                row = forces[(*spots[f // 4], slice(f % 4, f % 4 + 1), slice(None))]
                for p, piece in enumerate(split3(jnp.where(here, row, 0.0))):
                    pieces[p].append(piece)
            flag = jnp.where(here, 1.0, 0.0)
            blank = jnp.zeros_like(flag)
            lefts.append(jnp.concatenate(pieces[0] + pieces[1] + pieces[2] + [flag, blank], 0).astype(BF16))
        left = jnp.concatenate(lefts, 1)
        right = jnp.concatenate(rights, 1)
        total[...] += lax.dot_general(left, right, (((1,), (1,)), ((), ())), preferred_element_type=F32)
        return carry

    live = lax.fori_loop(0, rows, lambda q, n: n + counts[q, 1, 0], 0)
    lax.fori_loop(0, (live + PARTS - 1) // PARTS * (PARTS // together), one, 0)

    for order in range(7):
        if order < 6:
            parts = [total[(p * 6 + order) * highs : (p * 6 + order + 1) * highs, :] for p in range(3)]
            plane = parts[0] + parts[1] + parts[2]
        else:
            plane = total[18 * highs : 19 * highs, :]
        for c in range(highs):
            lined[order : order + 1, c * LANES : (c + 1) * LANES] = plane[c : c + 1, :]

    on = lined[6:7, :] > 0.5
    a1, k1 = lined[0:3, :], lined[3:6, :]
    x, v, a, k, dt = pos[...], vel[...], acc[...], jerk[...], step[...]
    v1 = v + 0.5 * dt * (a + a1) + dt * dt / 12.0 * (k - k1)
    x1 = x + 0.5 * dt * (v + v1) + dt * dt / 12.0 * (a - a1)
    new_pos[...] = jnp.where(on, x1, x)
    new_vel[...] = jnp.where(on, v1, v)
    new_acc[...] = jnp.where(on, a1, a)
    new_jerk[...] = jnp.where(on, k1, k)


def params(collective_id=None, limit=48 * 2**20):
    if collective_id is None:
        return pltpu.CompilerParams(vmem_limit_bytes=limit)
    return pltpu.CompilerParams(collective_id=collective_id, has_side_effects=True, vmem_limit_bytes=limit)


def per_device(positions, velocities, accels, jerks, masses, elapsed, active, live_tiles):
    rows = lax.axis_size("row")
    cols = lax.axis_size("col")
    width = positions.shape[1]
    tiles = active.shape[0] // TILE
    unit = TILE // PARTS
    blocks = 2 * rows
    cubes = rows * cols // PARTS
    share = blocks // cubes
    plane = cols // 2
    total_stars = width * rows * cols
    dma = pltpu.SemaphoreType.DMA

    live = jnp.arange(tiles)[:, None] < live_tiles[0]
    named = jnp.where(live, active.reshape(tiles, TILE), -1)
    parts = named.reshape(tiles, PARTS, unit).transpose(1, 0, 2).reshape(PARTS, 1, LANES)
    msg = jnp.concatenate([parts, jnp.broadcast_to(live_tiles[0], parts.shape)], 1)

    shard, ids = pl.pallas_call(
        functools.partial(gather_kernel, rows, cols, total_stars),
        out_shape=(
            jax.ShapeDtypeStruct((PARTS, 8, width), F32),
            jax.ShapeDtypeStruct((rows, 2, LANES), jnp.int32),
        ),
        in_specs=[vmem()] * 7,
        out_specs=(vmem(), vmem()),
        scratch_shapes=[dma for _ in range(4)],
        compiler_params=params(0),
        name="gather_shard",
    )(positions, velocities, accels, jerks, masses, elapsed, msg)

    picked, packed = pl.pallas_call(
        functools.partial(pick_kernel, rows, cols, width),
        out_shape=(
            jax.ShapeDtypeStruct((blocks, 4, LANES), F32),
            jax.ShapeDtypeStruct((rows + 4, 8, LANES), jnp.int32),
        ),
        in_specs=[smem(), vmem(), vmem()],
        out_specs=(vmem(), vmem()),
        scratch_shapes=[VMEM((6 * PARTS * width // LANES, 3 * LANES), BF16)],
        compiler_params=params(),
        name="pick_states",
    )(ids, shard, ids)

    states = pl.pallas_call(
        functools.partial(cube_sum_kernel, rows, cols),
        out_shape=jax.ShapeDtypeStruct((blocks, 4, LANES), F32),
        in_specs=[vmem()],
        out_specs=vmem(),
        scratch_shapes=[VMEM((cubes, share, 4, LANES), F32)] + [dma for _ in range(4)],
        compiler_params=params(1),
        name="share_states",
    )(picked)

    pair_count = rows * LANES * PARTS * width
    partial = pl.pallas_call(
        functools.partial(sweep_kernel, rows, cols),
        out_shape=jax.ShapeDtypeStruct((blocks, 4, LANES), F32),
        in_specs=[smem(), vmem(), vmem(), vmem()],
        out_specs=vmem(),
        scratch_shapes=[VMEM((64, PARTS * width), BF16), VMEM((32, PARTS * width), BF16)],
        compiler_params=params(),
        cost_estimate=pl.CostEstimate(flops=200 * pair_count, bytes_accessed=2**20, transcendentals=pair_count),
        name="pair_sums",
    )(ids, shard, packed, states)

    forces = pl.pallas_call(
        functools.partial(deliver_kernel, rows, cols),
        out_shape=jax.ShapeDtypeStruct((2, plane, rows, share, 4, LANES), F32),
        in_specs=[vmem()],
        out_specs=vmem(),
        scratch_shapes=[
            VMEM((cubes, share, 4, LANES), F32),
            VMEM((rows, share, 4, LANES), F32),
            pltpu.SemaphoreType.DMA((4,)),
            pltpu.SemaphoreType.DMA((4,)),
        ],
        compiler_params=params(2),
        name="deliver_forces",
    )(partial)

    return pl.pallas_call(
        functools.partial(finish_kernel, rows, cols),
        out_shape=tuple(jax.ShapeDtypeStruct((3, width), F32) for _ in range(4)),
        in_specs=[smem()] + [vmem()] * 6,
        out_specs=(vmem(),) * 4,
        scratch_shapes=[VMEM((20 * width // LANES, LANES), F32), VMEM((8, width), F32)],
        compiler_params=params(),
        name="finish_step",
    )(ids, forces, positions, velocities, accels, jerks, elapsed)


def solution(mesh):
    stars = P(None, ("row", "col"))
    in_specs = (stars,) * 6 + (P("row"), P("row"))
    return jax.shard_map(per_device, mesh=mesh, in_specs=in_specs, out_specs=(stars,) * 4, check_vma=False)
```

```python
import functools

import jax
import jax.numpy as jnp
from jax import lax
from jax.experimental import pallas as pl
from jax.experimental.pallas import tpu as pltpu
from jax.sharding import PartitionSpec as P

TILE = 128
EPS2 = 0.01
LANES = 128
BLOCK_J = 4096
PIECE_J = 1024
PARTS = 16
MESH = pl.DeviceIdType.MESH
VMEM = pltpu.VMEM
F32 = jnp.float32
BF16 = jnp.bfloat16


def vmem():
    return pl.BlockSpec(memory_space=pltpu.VMEM)


def smem():
    return pl.BlockSpec(memory_space=pltpu.SMEM)


def split3(x):
    high = x.astype(BF16).astype(F32)
    rest = x - high
    mid = rest.astype(BF16).astype(F32)
    return high, mid, rest - mid


class Place:
    def __init__(self, rows, cols):
        self.rows, self.cols = rows, cols
        self.side = {32: 4, 8: 2}[cols]
        self.half = self.side // 2
        self.quarters, self.layers = self.half * self.half, rows // 2
        self.cubes = self.quarters * self.layers
        self.row = lax.axis_index("row")
        self.col = lax.axis_index("col")
        self.y = self.col // (2 * self.side)
        self.x = lax.rem(self.col // 2, self.side)
        self.core = lax.rem(self.col, 2)
        self.quarter = self.y // 2 * self.half + self.x // 2
        self.layer = self.row // 2
        self.cube = self.quarter * self.layers + self.layer
        self.member = self.member_at(self.row)

    def member_at(self, row):
        return ((lax.rem(row, 2) * 2 + lax.rem(self.y, 2)) * 2 + lax.rem(self.x, 2)) * 2 + self.core

    def device(self, row, y, x, core):
        return {"row": row, "col": (y * self.side + x) * 2 + core}

    def in_cube(self, member):
        return self.device(
            self.layer * 2 + member // 8,
            self.y // 2 * 2 + lax.rem(member // 4, 2),
            self.x // 2 * 2 + lax.rem(member // 2, 2),
            lax.rem(member, 2),
        )

    def in_quarter(self, quarter):
        y = quarter // self.half * 2 + lax.rem(self.y, 2)
        x = lax.rem(quarter, self.half) * 2 + lax.rem(self.x, 2)
        return self.device(self.row, y, x, self.core)

    def in_layer(self, layer):
        return {"row": layer * 2 + lax.rem(self.row, 2)}


def signal(device):
    pl.semaphore_signal(pltpu.get_barrier_semaphore(), inc=1, device_id=device, device_id_type=MESH)


def await_greetings(count):
    pl.semaphore_wait(pltpu.get_barrier_semaphore(), count)


def each(first, last, body, step=1):
    def one(n, carry):
        body(first + n * step)
        return carry

    lax.fori_loop(0, (last - first + step - 1) // step, one, 0)


def remote(source, target, send, recv, device):
    return pltpu.make_async_remote_copy(
        src_ref=source, dst_ref=target, send_sem=send, recv_sem=recv, device_id=device, device_id_type=MESH
    )


def await_bytes(ref, semaphore):
    pltpu.make_async_copy(ref, ref, semaphore).wait()


def dots(tile):
    first = lax.broadcasted_iota(jnp.int32, tile.shape, 0) < 3
    swapped = pltpu.roll(tile, 4, 0)
    norm = jnp.sum(jnp.where(first, tile * tile, 0.0), axis=0, keepdims=True)
    cross = jnp.sum(jnp.where(first, tile * swapped, 0.0), axis=0, keepdims=True)
    return norm, cross


def cube_sums(at, blocks, from_quarters, from_layers, sends, recvs, meanwhile=None):
    share = blocks.shape[0] // at.cubes
    span = share * at.layers
    from_quarters[at.quarter] = blocks[pl.ds(at.quarter * span, span)]

    def to_quarter(d):
        quarter = lax.rem(at.quarter + d, at.quarters)
        part = blocks.at[pl.ds(quarter * span, span)]
        remote(part, from_quarters.at[at.quarter], sends.at[0], recvs.at[0], at.in_quarter(quarter)).start()

    rest_a = from_quarters.at[pl.ds(0, at.quarters - 1)]
    if at.quarters > 1:
        for d in range(1, at.quarters):
            to_quarter(d)
        await_bytes(rest_a, recvs.at[0])
    total = jnp.sum(from_quarters[...], axis=0)
    blocks[pl.ds(at.quarter * span, span)] = total
    from_layers[at.layer] = blocks[pl.ds(at.cube * share, share)]

    def to_layer(d):
        layer = lax.rem(at.layer + d, at.layers)
        part = blocks.at[pl.ds((at.quarter * at.layers + layer) * share, share)]
        remote(part, from_layers.at[at.layer], sends.at[1], recvs.at[1], at.in_layer(layer)).start()

    for d in range(1, at.layers):
        to_layer(d)
    if meanwhile is not None:
        meanwhile()
    rest_b = from_layers.at[pl.ds(0, at.layers - 1)]
    await_bytes(rest_b, recvs.at[1])
    left = [(rest_b, sends.at[1])]
    if at.quarters > 1:
        left.append((rest_a, sends.at[0]))
    return jnp.sum(from_layers[...], axis=0), left


def gather_kernel(
    rows,
    cols,
    total_stars,
    pos,
    vel,
    acc,
    jerk,
    mass,
    step,
    msg,
    ids,
    states,
    j_side,
    j_mass,
    shard,
    picked,
    from_quarters,
    from_layers,
    table,
    sends,
    recvs,
):
    at = Place(rows, cols)
    me, mine, cubes = at.member, at.cube, at.cubes
    share = states.shape[0] // cubes
    for d in range(1, at.quarters):
        signal(at.in_quarter(lax.rem(at.quarter + d, at.quarters)))
    each(1, rows, lambda d: signal({"row": lax.rem(at.row + d, rows)}))
    each(1, PARTS, lambda d: signal(at.in_cube(lax.rem(me + d, PARTS))))
    dt = step[...]
    a, j, v = acc[...], jerk[...], vel[...]
    shard[me, 0:3, :] = pos[...] + dt * (v + dt * (0.5 * a + dt * j / 6.0))
    shard[me, 3:4, :] = mass[...] / total_stars
    shard[me, 4:7, :] = v + dt * (a + dt * (0.5 * j))
    shard[me, 7:8, :] = jnp.ones_like(dt)
    ids[at.row] = msg[me]
    await_greetings(PARTS - 1 + rows - 1 + at.quarters - 1)

    def send_ids(d):
        peer = lax.rem(at.row + d, rows)
        remote(msg.at[at.member_at(peer)], ids.at[at.row], sends.at[4], recvs.at[4], {"row": peer}).start()

    def send_block(d):
        peer = lax.rem(me + d, PARTS)
        remote(shard.at[me], shard.at[me], sends.at[5], recvs.at[5], at.in_cube(peer)).start()

    each(1, PARTS, send_block)
    each(1, rows, send_ids)
    id_rest, shard_rest = ids.at[pl.ds(0, rows - 1)], shard.at[pl.ds(0, PARTS - 1)]
    await_bytes(shard_rest, recvs.at[5])
    await_bytes(id_rest, recvs.at[4])

    width = pos.shape[1]
    chunks = width // LANES
    high_count = PARTS * chunks
    features = (0, 1, 2, 4, 5, 6)
    groups = min(4, rows)
    for order, f in enumerate(features):
        plane = jnp.concatenate([shard[:, f, c * LANES : (c + 1) * LANES] for c in range(chunks)], 0)
        h, m, l = split3(plane)
        table[order * high_count : (order + 1) * high_count, :] = jnp.concatenate([h, m, l], 1).astype(BF16)
    picked[...] = jnp.zeros_like(picked)

    def part(g, carry):
        first = g * groups
        star = jnp.concatenate([ids[first + n, 0:1, :] for n in range(groups)], 1)
        owner = star // width
        row, col = owner // cols, lax.rem(owner, cols)
        y, x = col // (2 * at.side), lax.rem(col // 2, at.side)
        cube = (y // 2 * at.half + x // 2) * at.layers + row // 2
        member = ((lax.rem(row, 2) * 2 + lax.rem(y, 2)) * 2 + lax.rem(x, 2)) * 2 + lax.rem(col, 2)
        place = lax.rem(star, width)
        high = jnp.where((star >= 0) & (cube == mine), place // LANES * PARTS + member, -1)
        low = lax.rem(place, LANES)
        span = groups * LANES
        pick = jnp.where(lax.broadcasted_iota(jnp.int32, (LANES, span), 0) == low, 1.0, 0.0).astype(BF16)
        pick = jnp.concatenate([pick, pick, pick], 0)
        at_row = lax.broadcasted_iota(jnp.int32, (high_count, span), 0) == high
        for order, f in enumerate(features):
            values = jnp.dot(table[order * high_count : (order + 1) * high_count, :], pick, preferred_element_type=F32)
            found = jnp.sum(jnp.where(at_row, values, 0.0), axis=0, keepdims=True)
            for n in range(groups):
                picked[2 * (first + n) + f // 4, f % 4 : f % 4 + 1, :] = found[:, n * LANES : (n + 1) * LANES]
        return carry

    lax.fori_loop(0, rows // groups, part, 0)

    def prepare(z, carry):
        tile = shard[z]
        norm, cross = dots(tile)
        h, m, l = split3(tile)
        pieces = split3(norm) + split3(cross)
        line = lax.broadcasted_iota(jnp.int32, tile.shape, 0)
        extra = jnp.zeros_like(tile)
        for n, piece in enumerate(pieces):
            extra = jnp.where(line == n, piece, extra)
        blank = jnp.zeros((LANES - 56, width), F32)
        side = jnp.concatenate([h, h, h, m, m, l, extra, blank], 0)
        for c in range(chunks):
            place = pl.ds(pl.multiple_of(z * width + c * LANES, LANES), LANES)
            j_side[place, :] = side[:, c * LANES : (c + 1) * LANES].T.astype(BF16)
        h, m, l = split3(tile * tile[3:4, :])
        place = pl.ds(pl.multiple_of(z * width, width), width)
        j_mass[:, place] = jnp.concatenate([h, m, l, jnp.zeros_like(tile)], 0).astype(BF16)
        return carry

    total, left = cube_sums(
        at, picked, from_quarters, from_layers, sends, recvs, lambda: lax.fori_loop(0, PARTS // 2, prepare, 0)
    )
    own = pl.ds(mine * share, share)
    states[own] = total
    for d in range(1, at.layers):
        layer = lax.rem(at.layer + d, at.layers)
        remote(states.at[own], states.at[own], sends.at[2], recvs.at[2], at.in_layer(layer)).start()
    lax.fori_loop(PARTS // 2, PARTS, prepare, 0)
    rest = states.at[pl.ds(0, (at.layers - 1) * share)]
    await_bytes(rest, recvs.at[2])
    left.append((rest, sends.at[2]))
    span = at.layers * share
    quarter = pl.ds(at.quarter * span, span)
    if at.quarters > 1:
        for d in range(1, at.quarters):
            device = at.in_quarter(lax.rem(at.quarter + d, at.quarters))
            remote(states.at[quarter], states.at[quarter], sends.at[3], recvs.at[3], device).start()
        rest = states.at[pl.ds(0, (at.quarters - 1) * span)]
        await_bytes(rest, recvs.at[3])
        left.append((rest, sends.at[3]))
    left += [(id_rest, sends.at[4]), (shard_rest, sends.at[5])]
    for ref, semaphore in left:
        await_bytes(ref, semaphore)


def sweep_kernel(rows, cols, counts, ids, states, j_side, j_mass, out, i_tiles):
    at = Place(rows, cols)
    total = j_side.shape[0]
    at8 = lax.broadcasted_iota(jnp.int32, (8, LANES), 0)
    lane = lax.broadcasted_iota(jnp.int32, (8, LANES), 1)
    out[...] = jnp.zeros_like(out)
    i_tiles[...] = jnp.where(lax.broadcasted_iota(jnp.int32, i_tiles.shape, 1) == 3, -1.0, 0.0)

    def pack(q, offset):
        tile = jnp.concatenate([states[2 * q], states[2 * q + 1]], 0)
        tile = jnp.where(at8 == 3, ids[q, 0:1, :].astype(F32), tile)
        t, shift = offset // LANES, lax.rem(offset, LANES)
        rolled = pltpu.roll(tile, shift, 1)
        i_tiles[t] = jnp.where(lane >= shift, rolled, i_tiles[t])
        i_tiles[t + 1] = jnp.where(lane < shift, rolled, i_tiles[t + 1])
        return offset + counts[q, 1, 0] * (TILE // PARTS)

    used = lax.fori_loop(0, rows, pack, 0)

    def right_of(tile):
        norm, cross = dots(tile)
        h, m, l = split3(tile)
        nh, nm, nl = split3(norm + EPS2)
        ch, cm, cl = split3(cross)

        def for_r(piece, last):
            return jnp.where(at8 < 3, -2.0 * piece, jnp.where(at8 == 7, last, 0.0))

        def for_b(piece, last):
            return jnp.where(at8 == 7, last, jnp.where(at8 == 3, 0.0, -pltpu.roll(piece, 4, 0)))

        r_extra = jnp.where(at8 < 3, 1.0, 0.0)
        b_extra = jnp.where((at8 >= 3) & (at8 < 6), 1.0, 0.0)
        blank = jnp.zeros((LANES - 56, LANES), F32)
        right_r = jnp.concatenate(
            [for_r(h, nh), for_r(m, nm), for_r(l, nl), for_r(h, 0.0), for_r(m, 0.0), for_r(h, 0.0), r_extra, blank], 0
        )
        right_b = jnp.concatenate(
            [for_b(h, ch), for_b(m, cm), for_b(l, cl), for_b(h, 0.0), for_b(m, 0.0), for_b(h, 0.0), b_extra, blank], 0
        )
        return jnp.concatenate([right_r, right_b], 1).astype(BF16)

    def run(t, carry):
        tile = i_tiles[t]
        right = right_of(tile)

        def one_block(n, sums):
            def place(s):
                return pl.ds(pl.multiple_of(n * BLOCK_J + s * PIECE_J, PIECE_J), PIECE_J)

            def distances(s):
                return jnp.dot(j_side[place(s), :], right, preferred_element_type=F32)

            ahead = distances(0)
            for s in range(BLOCK_J // PIECE_J):
                both = ahead
                if s + 1 < BLOCK_J // PIECE_J:
                    ahead = distances(s + 1)
                inverse = lax.rsqrt(both[:, 0:LANES])
                square = inverse * inverse
                near = square * inverse
                tilt = near * square * both[:, LANES:]
                pair = jnp.concatenate([near, tilt], 1)
                high = pair.astype(BF16)
                low = (pair - high.astype(F32)).astype(BF16)
                weights = j_mass[:, place(s)]
                sums += jnp.dot(
                    jnp.concatenate([weights, weights], 1),
                    jnp.concatenate([high, low], 0),
                    preferred_element_type=F32,
                )
            return sums

        sums = lax.fori_loop(0, total // BLOCK_J, one_block, jnp.zeros((32, 2 * LANES), F32))
        sums = sums[0:8] + sums[8:16] + sums[16:24]
        near, tilt = sums[:, 0:LANES], sums[:, LANES:]
        near = near - tile * near[7:8]
        tilt = tilt - tile * tilt[7:8]
        force = near - jnp.where(at8 >= 4, 3.0 * pltpu.roll(tilt, 4, 0), 0.0)
        star = tile[3:4]
        force = jnp.where(star >= 0, force, 0.0)
        force = jnp.where(at8 == 3, jnp.where(at.cube == 0, star, 0.0), force)
        out[2 * t] = force[0:4]
        out[2 * t + 1] = force[4:8]
        return carry

    lax.fori_loop(0, (used + LANES - 1) // LANES, run, 0)


def deliver_kernel(rows, cols, partial, out, blocks, from_quarters, from_layers, lined, sends, recvs, plane_recv):
    at = Place(rows, cols)
    side = at.side
    plane = side * side
    here = at.y * side + at.x
    sibling = at.device(at.row, at.y, at.x, 1 - at.core)

    def beside(d):
        spot = lax.rem(here + d, plane)
        return at.device(at.row, spot // side, lax.rem(spot, side), at.core)

    each(1, rows, lambda d: signal({"row": lax.rem(at.row + d, rows)}))
    each(1, plane, lambda d: signal(beside(d)))
    signal(sibling)
    blocks[...] = partial[...]
    await_greetings(rows - 1 + plane)

    total, left = cube_sums(at, blocks, from_quarters, from_layers, sends, recvs)
    lined[at.row] = total
    mine = lined.at[at.row]
    for d in range(1, rows):
        remote(mine, mine, sends.at[2], recvs.at[2], {"row": lax.rem(at.row + d, rows)}).start()
    line = lined.at[pl.ds(0, rows - 1)]
    await_bytes(line, recvs.at[2])

    def across(d):
        return remote(lined, out.at[at.core, here], sends.at[3], plane_recv.at[d], beside(d))

    each(1, plane, lambda d: across(d).start())
    remote(lined, out.at[at.core, here], sends.at[4], recvs.at[4], sibling).start()
    out[at.core, here] = lined[...]

    def forward(d):
        block = out.at[at.core, lax.rem(here - d + plane, plane)]
        remote(lined, block, sends.at[3], plane_recv.at[d], beside(d)).wait_recv()
        remote(block, block, sends.at[4], recvs.at[4], sibling).start()

    each(1, plane, forward)
    await_bytes(out.at[0], recvs.at[4])
    left += [(line, sends.at[2]), (out.at[0, pl.ds(0, plane - 1)], sends.at[3]), (out.at[0], sends.at[4])]
    for ref, semaphore in left:
        await_bytes(ref, semaphore)


def finish_kernel(
    rows, cols, counts, forces, pos, vel, acc, jerk, step, new_pos, new_vel, new_acc, new_jerk, total, lined
):
    at = Place(rows, cols)
    width = pos.shape[1]
    highs = width // LANES
    mine = at.row * cols + at.col
    features = (0, 1, 2, 4, 5, 6)
    share = forces.shape[3]
    together = 8
    at8 = lax.broadcasted_iota(jnp.int32, (highs, LANES), 0)
    at_low = lax.broadcasted_iota(jnp.int32, (LANES, LANES), 0)
    total[...] = jnp.zeros_like(total)

    def one(n, carry):
        t, first = n // (PARTS // together), lax.rem(n, PARTS // together) * together
        lefts, rights = [], []
        for k in range(together):
            member = first + k
            spots = []
            for b in range(2):
                cube = (2 * t + b) // share
                quarter = cube // at.layers
                z = lax.rem(cube, at.layers) * 2 + member // 8
                y = quarter // at.half * 2 + lax.rem(member // 4, 2)
                x = lax.rem(quarter, at.half) * 2 + lax.rem(member // 2, 2)
                spots.append((lax.rem(member, 2), y * at.side + x, z, lax.rem(2 * t + b, share)))
            star = forces[(*spots[0], slice(3, 4), slice(None))].astype(jnp.int32)
            ok = (star >= 0) & (star // width == mine)
            place = lax.rem(star, width)
            here = jnp.where(ok, place // LANES, -1) == at8
            low = lax.rem(place, LANES)
            rights.append(jnp.where(at_low == low, 1.0, 0.0).astype(BF16))
            pieces = [[], [], []]
            for f in features:
                row = forces[(*spots[f // 4], slice(f % 4, f % 4 + 1), slice(None))]
                for p, piece in enumerate(split3(jnp.where(here, row, 0.0))):
                    pieces[p].append(piece)
            flag = jnp.where(here, 1.0, 0.0)
            blank = jnp.zeros_like(flag)
            lefts.append(jnp.concatenate(pieces[0] + pieces[1] + pieces[2] + [flag, blank], 0).astype(BF16))
        left = jnp.concatenate(lefts, 1)
        right = jnp.concatenate(rights, 1)
        total[...] += lax.dot_general(left, right, (((1,), (1,)), ((), ())), preferred_element_type=F32)
        return carry

    live = lax.fori_loop(0, rows, lambda q, n: n + counts[q, 1, 0], 0)
    lax.fori_loop(0, (live + PARTS - 1) // PARTS * (PARTS // together), one, 0)

    for order in range(7):
        if order < 6:
            parts = [total[(p * 6 + order) * highs : (p * 6 + order + 1) * highs, :] for p in range(3)]
            plane = parts[0] + parts[1] + parts[2]
        else:
            plane = total[18 * highs : 19 * highs, :]
        for c in range(highs):
            lined[order : order + 1, c * LANES : (c + 1) * LANES] = plane[c : c + 1, :]

    on = lined[6:7, :] > 0.5
    a1, k1 = lined[0:3, :], lined[3:6, :]
    x, v, a, k, dt = pos[...], vel[...], acc[...], jerk[...], step[...]
    v1 = v + 0.5 * dt * (a + a1) + dt * dt / 12.0 * (k - k1)
    x1 = x + 0.5 * dt * (v + v1) + dt * dt / 12.0 * (a - a1)
    new_pos[...] = jnp.where(on, x1, x)
    new_vel[...] = jnp.where(on, v1, v)
    new_acc[...] = jnp.where(on, a1, a)
    new_jerk[...] = jnp.where(on, k1, k)


def params(collective_id=None, limit=32 * 2**20):
    if collective_id is None:
        return pltpu.CompilerParams(vmem_limit_bytes=limit)
    return pltpu.CompilerParams(collective_id=collective_id, has_side_effects=True, vmem_limit_bytes=limit)


def per_device(positions, velocities, accels, jerks, masses, elapsed, active, live_tiles):
    rows = lax.axis_size("row")
    cols = lax.axis_size("col")
    width = positions.shape[1]
    tiles = active.shape[0] // TILE
    unit = TILE // PARTS
    blocks = 2 * rows
    cubes = rows * cols // PARTS
    share = blocks // cubes
    plane = cols // 2
    total_stars = width * rows * cols

    live = jnp.arange(tiles)[:, None] < live_tiles[0]
    named = jnp.where(live, active.reshape(tiles, TILE), -1)
    parts = named.reshape(tiles, PARTS, unit).transpose(1, 0, 2).reshape(PARTS, 1, LANES)
    msg = jnp.concatenate([parts, jnp.broadcast_to(live_tiles[0], parts.shape)], 1)

    quarters, layers = cols // 8, rows // 2
    cube_scratch = [
        VMEM((blocks, 4, LANES), F32),
        VMEM((quarters, layers * share, 4, LANES), F32),
        VMEM((layers, share, 4, LANES), F32),
    ]
    dma = pltpu.SemaphoreType.DMA

    ids, states, j_side, j_mass = pl.pallas_call(
        functools.partial(gather_kernel, rows, cols, total_stars),
        out_shape=(
            jax.ShapeDtypeStruct((rows, 2, LANES), jnp.int32),
            jax.ShapeDtypeStruct((blocks, 4, LANES), F32),
            jax.ShapeDtypeStruct((PARTS * width, LANES), BF16),
            jax.ShapeDtypeStruct((32, PARTS * width), BF16),
        ),
        in_specs=[vmem()] * 7,
        out_specs=(vmem(),) * 4,
        scratch_shapes=[VMEM((PARTS, 8, width), F32)]
        + cube_scratch
        + [VMEM((6 * PARTS * width // LANES, 3 * LANES), BF16), dma((6,)), dma((6,))],
        compiler_params=params(0),
        name="gather_states",
    )(positions, velocities, accels, jerks, masses, elapsed, msg)

    pair_count = rows * LANES * PARTS * width
    partial = pl.pallas_call(
        functools.partial(sweep_kernel, rows, cols),
        out_shape=jax.ShapeDtypeStruct((blocks, 4, LANES), F32),
        in_specs=[smem()] + [vmem()] * 4,
        out_specs=vmem(),
        scratch_shapes=[VMEM((rows + 2, 8, LANES), F32)],
        compiler_params=params(),
        cost_estimate=pl.CostEstimate(flops=200 * pair_count, bytes_accessed=2**20, transcendentals=pair_count),
        name="pair_sums",
    )(ids, ids, states, j_side, j_mass)

    forces = pl.pallas_call(
        functools.partial(deliver_kernel, rows, cols),
        out_shape=jax.ShapeDtypeStruct((2, plane, rows, share, 4, LANES), F32),
        in_specs=[vmem()],
        out_specs=vmem(),
        scratch_shapes=cube_scratch + [VMEM((rows, share, 4, LANES), F32), dma((5,)), dma((5,)), dma((plane,))],
        compiler_params=params(1),
        name="deliver_forces",
    )(partial)

    return pl.pallas_call(
        functools.partial(finish_kernel, rows, cols),
        out_shape=tuple(jax.ShapeDtypeStruct((3, width), F32) for _ in range(4)),
        in_specs=[smem()] + [vmem()] * 6,
        out_specs=(vmem(),) * 4,
        scratch_shapes=[VMEM((20 * width // LANES, LANES), F32), VMEM((8, width), F32)],
        compiler_params=params(),
        name="finish_step",
    )(ids, forces, positions, velocities, accels, jerks, elapsed)


def solution(mesh):
    stars = P(None, ("row", "col"))
    in_specs = (stars,) * 6 + (P("row"), P("row"))
    return jax.shard_map(per_device, mesh=mesh, in_specs=in_specs, out_specs=(stars,) * 4, check_vma=False)
```

```python
import functools

import jax
import jax.numpy as jnp
from jax import lax
from jax.experimental import pallas as pl
from jax.experimental.pallas import tpu as pltpu
from jax.sharding import PartitionSpec as P

TILE = 128
EPS2 = 0.01
LANES = 128
BLOCK_J = 4096
PIECE_J = 256
PARTS = 16
MESH = pl.DeviceIdType.MESH
VMEM = pltpu.VMEM
F32 = jnp.float32
BF16 = jnp.bfloat16


def anywhere():
    return pl.BlockSpec(memory_space=pl.ANY)


def vmem():
    return pl.BlockSpec(memory_space=pltpu.VMEM)


def smem():
    return pl.BlockSpec(memory_space=pltpu.SMEM)


def split3(x):
    high = x.astype(BF16).astype(F32)
    rest = x - high
    mid = rest.astype(BF16).astype(F32)
    return high, mid, rest - mid


class Place:
    def __init__(self, rows, cols):
        self.rows, self.cols = rows, cols
        self.side = {32: 4, 8: 2, 2: 1}[cols]
        self.plane, self.layers = self.side * self.side, rows // 2
        self.groups = 2 * self.plane
        self.row = lax.axis_index("row")
        self.col = lax.axis_index("col")
        self.spot, self.core = self.col // 2, lax.rem(self.col, 2)
        self.parity, self.layer = lax.rem(self.row, 2), self.row // 2
        self.group = self.parity * self.plane + self.spot
        self.member = self.layer * 2 + self.core
        self.sibling = {"col": self.spot * 2 + 1 - self.core}
        self.twin = {"row": self.layer * 2 + 1 - self.parity}

    def in_layer(self, layer):
        return {"row": layer * 2 + self.parity}

    def at_spot(self, spot):
        return {"col": spot * 2 + self.core}


def signal(device):
    pl.semaphore_signal(pltpu.get_barrier_semaphore(), inc=1, device_id=device, device_id_type=MESH)


def await_greetings(count):
    pl.semaphore_wait(pltpu.get_barrier_semaphore(), count)


def each(first, last, body, step=1):
    def one(n, carry):
        body(first + n * step)
        return carry

    lax.fori_loop(0, (last - first + step - 1) // step, one, 0)


def remote(source, target, send, recv, device):
    return pltpu.make_async_remote_copy(
        src_ref=source, dst_ref=target, send_sem=send, recv_sem=recv, device_id=device, device_id_type=MESH
    )


def await_bytes(ref, semaphore):
    pltpu.make_async_copy(ref, ref, semaphore).wait()


def dots(tile):
    first = lax.broadcasted_iota(jnp.int32, tile.shape, 0) < 3
    swapped = pltpu.roll(tile, 4, 0)
    norm = jnp.sum(jnp.where(first, tile * tile, 0.0), axis=0, keepdims=True)
    cross = jnp.sum(jnp.where(first, tile * swapped, 0.0), axis=0, keepdims=True)
    return norm, cross


def group_sums(at, blocks, from_twin, from_spots, sends, recvs, meanwhile=None):
    share = blocks.shape[0] // at.groups
    span = share * at.plane
    theirs = blocks.at[pl.ds((1 - at.parity) * span, span)]
    remote(theirs, from_twin, sends.at[0], recvs.at[0], at.twin).start()
    mine = pl.ds(at.parity * span, span)
    await_bytes(from_twin, recvs.at[0])
    blocks[mine] = blocks[mine] + from_twin[...]
    from_spots[at.spot] = blocks[pl.ds(at.group * share, share)]

    def to_spot(d):
        spot = lax.rem(at.spot + d, at.plane)
        part = blocks.at[pl.ds(at.parity * span + spot * share, share)]
        remote(part, from_spots.at[at.spot], sends.at[1], recvs.at[1], at.at_spot(spot)).start()

    left = [(from_twin, sends.at[0])]
    if at.plane > 1:
        for d in range(1, at.plane):
            to_spot(d)
        if meanwhile is not None:
            meanwhile()
        rest = from_spots.at[pl.ds(0, at.plane - 1)]
        await_bytes(rest, recvs.at[1])
        left.append((rest, sends.at[1]))
    elif meanwhile is not None:
        meanwhile()
    return jnp.sum(from_spots[...], axis=0), left


def gather_kernel(
    rows,
    cols,
    total_stars,
    pos_in,
    vel_in,
    acc_in,
    jerk_in,
    mass_in,
    step_in,
    msg,
    ids,
    states,
    j_side,
    j_mass,
    shard,
    picked,
    from_twin,
    from_spots,
    table,
    pos,
    vel,
    acc,
    jerk,
    mass,
    step,
    loads,
    sends,
    recvs,
    id_send,
    id_recv,
    right_recv,
    left_recv,
    core_recv,
):
    at = Place(rows, cols)
    me, mine, layers = at.member, at.group, at.layers
    share = states.shape[0] // at.groups
    pairs = ((pos_in, pos), (vel_in, vel), (acc_in, acc), (jerk_in, jerk), (mass_in, mass), (step_in, step))
    loading = [pltpu.make_async_copy(source, target, loads.at[n]) for n, (source, target) in enumerate(pairs)]
    for load in loading:
        load.start()
    signal(at.sibling)
    for d in range(1, rows):
        signal({"row": lax.rem(at.row + d, rows)})
    for d in range(1, at.plane):
        signal(at.at_spot(lax.rem(at.spot + d, at.plane)))
    ids[at.row] = msg[me]
    for load in loading:
        load.wait()
    dt = step[...]
    a, j, v = acc[...], jerk[...], vel[...]
    shard[me, 0:3, :] = pos[...] + dt * (v + dt * (0.5 * a + dt * j / 6.0))
    shard[me, 3:4, :] = mass[...] / total_stars
    shard[me, 4:7, :] = v + dt * (a + dt * (0.5 * j))
    shard[me, 7:8, :] = jnp.ones_like(dt)
    await_greetings(rows + at.plane - 1)

    width = pos.shape[1]
    chunks = width // LANES

    def prepare(z):
        tile = shard[z]
        norm, cross = dots(tile)
        h, m, l = split3(tile)
        pieces = split3(norm) + split3(cross)
        line = lax.broadcasted_iota(jnp.int32, tile.shape, 0)
        extra = jnp.zeros_like(tile)
        for n, piece in enumerate(pieces):
            extra = jnp.where(line == n, piece, extra)
        blank = jnp.zeros((LANES - 56, width), F32)
        side = jnp.concatenate([h, h, h, m, m, l, extra, blank], 0)
        for c in range(chunks):
            place = pl.ds(pl.multiple_of(z * width + c * LANES, LANES), LANES)
            j_side[place, :] = side[:, c * LANES : (c + 1) * LANES].T.astype(BF16)
        h, m, l = split3(tile * tile[3:4, :])
        place = pl.ds(pl.multiple_of(z * width, width), width)
        j_mass[:, place] = jnp.concatenate([h, m, l, jnp.zeros_like(tile)], 0).astype(BF16)

    def prepare_layers(s, both):
        def one(n):
            layer = lax.rem(at.layer + (n // 2 * 2 - 1) * s + layers, layers)
            prepare(layer * 2 + lax.rem(n, 2))

        each(0, 4 if both else 2, one)

    def ring(s, way):
        block = shard.at[lax.rem(at.layer - way * s + layers, layers) * 2 + at.core]
        recv = (right_recv if way > 0 else left_recv).at[s]
        return remote(block, block, sends.at[4], recv, at.in_layer(lax.rem(at.layer + way + layers, layers)))

    def arrived(s, way):
        block = shard.at[lax.rem(at.layer - way * (s + 1) + 2 * layers, layers) * 2 + at.core]
        recv = (right_recv if way > 0 else left_recv).at[s]
        remote(block, block, sends.at[4], recv, at.in_layer(lax.rem(at.layer + way + layers, layers))).wait_recv()

    def across(s, way, core):
        block = shard.at[lax.rem(at.layer - way * s + layers, layers) * 2 + core]
        return remote(block, block, sends.at[5], core_recv.at[2 * s + (1 - way) // 2], at.sibling)

    ways = (layers // 2, layers - 1 - layers // 2)
    for s in range(ways[0] + 1):
        if s < ways[0]:
            ring(s, 1).start()
        if s < ways[1]:
            ring(s, -1).start()
        across(s, 1, at.core).start()
        if 0 < s <= ways[1]:
            across(s, -1, at.core).start()
        if s == 0:

            def send_ids(d):
                peer = lax.rem(at.row + d, rows)
                part = msg.at[peer // 2 * 2 + at.core]
                remote(part, ids.at[at.row], id_send, id_recv, {"row": peer}).start()

            each(1, rows, send_ids)
        else:
            across(s - 1, 1, 1 - at.core).wait_recv()
            if 0 < s - 1 <= ways[1]:
                across(s - 1, -1, 1 - at.core).wait_recv()
            if s < ways[0]:
                prepare_layers(s - 1, 0 < s - 1 <= ways[1])
        if s < ways[0]:
            arrived(s, 1)
        if s < ways[1]:
            arrived(s, -1)
    across(ways[0], 1, 1 - at.core).wait_recv()
    id_rest = ids.at[pl.ds(0, rows - 1)]
    await_bytes(id_rest, id_recv)

    high_count = PARTS * chunks
    features = (0, 1, 2, 4, 5, 6)
    groups = min(4, rows)
    for order, f in enumerate(features):
        plane = jnp.concatenate([shard[:, f, c * LANES : (c + 1) * LANES] for c in range(chunks)], 0)
        h, m, l = split3(plane)
        table[order * high_count : (order + 1) * high_count, :] = jnp.concatenate([h, m, l], 1).astype(BF16)
    picked[...] = jnp.zeros_like(picked)

    def part(g, carry):
        first = g * groups
        star = jnp.concatenate([ids[first + n, 0:1, :] for n in range(groups)], 1)
        owner = star // width
        row, col = owner // cols, lax.rem(owner, cols)
        group = lax.rem(row, 2) * at.plane + col // 2
        member = row // 2 * 2 + lax.rem(col, 2)
        place = lax.rem(star, width)
        high = jnp.where((star >= 0) & (group == mine), place // LANES * PARTS + member, -1)
        low = lax.rem(place, LANES)
        span = groups * LANES
        pick = jnp.where(lax.broadcasted_iota(jnp.int32, (LANES, span), 0) == low, 1.0, 0.0).astype(BF16)
        pick = jnp.concatenate([pick, pick, pick], 0)
        at_row = lax.broadcasted_iota(jnp.int32, (high_count, span), 0) == high
        for order, f in enumerate(features):
            values = jnp.dot(table[order * high_count : (order + 1) * high_count, :], pick, preferred_element_type=F32)
            found = jnp.sum(jnp.where(at_row, values, 0.0), axis=0, keepdims=True)
            for n in range(groups):
                picked[2 * (first + n) + f // 4, f % 4 : f % 4 + 1, :] = found[:, n * LANES : (n + 1) * LANES]
        return carry

    lax.fori_loop(0, rows // groups, part, 0)

    late = ways[0] - 1

    def first_rest():
        prepare_layers(late, 0 < late <= ways[1])

    total, left = group_sums(at, picked, from_twin, from_spots, sends, recvs, first_rest)
    own = pl.ds(mine * share, share)
    states[own] = total
    span = at.plane * share
    half = pl.ds(at.parity * span, span)
    for d in range(1, at.plane):
        spot = lax.rem(at.spot + d, at.plane)
        remote(states.at[own], states.at[own], sends.at[2], recvs.at[2], at.at_spot(spot)).start()
    prepare_layers(ways[0], False)
    if at.plane > 1:
        rest = states.at[pl.ds(0, span - share)]
        await_bytes(rest, recvs.at[2])
        left.append((rest, sends.at[2]))
    remote(states.at[half], states.at[half], sends.at[3], recvs.at[3], at.twin).start()
    await_bytes(states.at[half], recvs.at[3])
    left += [
        (states.at[half], sends.at[3]),
        (shard.at[pl.ds(0, layers - 1)], sends.at[4]),
        (shard.at[pl.ds(0, layers)], sends.at[5]),
        (id_rest, id_send),
    ]
    for ref, semaphore in left:
        await_bytes(ref, semaphore)


def sweep_kernel(rows, cols, counts, ids, states, j_side, j_mass, out, i_tiles):
    at = Place(rows, cols)
    total = j_side.shape[0]
    at8 = lax.broadcasted_iota(jnp.int32, (8, LANES), 0)
    lane = lax.broadcasted_iota(jnp.int32, (8, LANES), 1)
    out[...] = jnp.zeros_like(out)
    i_tiles[...] = jnp.where(lax.broadcasted_iota(jnp.int32, i_tiles.shape, 1) == 3, -1.0, 0.0)

    def pack(q, offset):
        tile = jnp.concatenate([states[2 * q], states[2 * q + 1]], 0)
        tile = jnp.where(at8 == 3, ids[q, 0:1, :].astype(F32), tile)
        t, shift = offset // LANES, lax.rem(offset, LANES)
        rolled = pltpu.roll(tile, shift, 1)
        i_tiles[t] = jnp.where(lane >= shift, rolled, i_tiles[t])
        i_tiles[t + 1] = jnp.where(lane < shift, rolled, i_tiles[t + 1])
        return offset + counts[q, 1, 0] * (TILE // PARTS)

    used = lax.fori_loop(0, rows, pack, 0)

    def right_of(tile):
        norm, cross = dots(tile)
        h, m, l = split3(tile)
        nh, nm, nl = split3(norm + EPS2)
        ch, cm, cl = split3(cross)

        def for_r(piece, last):
            return jnp.where(at8 < 3, -2.0 * piece, jnp.where(at8 == 7, last, 0.0))

        def for_b(piece, last):
            return jnp.where(at8 == 7, last, jnp.where(at8 == 3, 0.0, -pltpu.roll(piece, 4, 0)))

        r_extra = jnp.where(at8 < 3, 1.0, 0.0)
        b_extra = jnp.where((at8 >= 3) & (at8 < 6), 1.0, 0.0)
        blank = jnp.zeros((LANES - 56, LANES), F32)
        right_r = jnp.concatenate(
            [for_r(h, nh), for_r(m, nm), for_r(l, nl), for_r(h, 0.0), for_r(m, 0.0), for_r(h, 0.0), r_extra, blank], 0
        )
        right_b = jnp.concatenate(
            [for_b(h, ch), for_b(m, cm), for_b(l, cl), for_b(h, 0.0), for_b(m, 0.0), for_b(h, 0.0), b_extra, blank], 0
        )
        return jnp.concatenate([right_r, right_b], 1).astype(BF16)

    def run(t, carry):
        tile = i_tiles[t]
        right = right_of(tile)

        def one_block(n, sums):
            def place(s):
                return pl.ds(pl.multiple_of(n * BLOCK_J + s * PIECE_J, PIECE_J), PIECE_J)

            def distances(s):
                return jnp.dot(j_side[place(s), :], right, preferred_element_type=F32)

            ahead = distances(0)
            for s in range(BLOCK_J // PIECE_J):
                both = ahead
                if s + 1 < BLOCK_J // PIECE_J:
                    ahead = distances(s + 1)
                inverse = lax.rsqrt(both[:, 0:LANES])
                square = inverse * inverse
                near = square * inverse
                tilt = near * square * both[:, LANES:]
                pair = jnp.concatenate([near, tilt], 1)
                high = pair.astype(BF16)
                low = (pair - high.astype(F32)).astype(BF16)
                weights = j_mass[:, place(s)]
                sums += jnp.dot(
                    jnp.concatenate([weights, weights], 1),
                    jnp.concatenate([high, low], 0),
                    preferred_element_type=F32,
                )
            return sums

        sums = lax.fori_loop(0, total // BLOCK_J, one_block, jnp.zeros((32, 2 * LANES), F32))
        sums = sums[0:8] + sums[8:16] + sums[16:24]
        near, tilt = sums[:, 0:LANES], sums[:, LANES:]
        near = near - tile * near[7:8]
        tilt = tilt - tile * tilt[7:8]
        force = near - jnp.where(at8 >= 4, 3.0 * pltpu.roll(tilt, 4, 0), 0.0)
        star = tile[3:4]
        force = jnp.where(star >= 0, force, 0.0)
        force = jnp.where(at8 == 3, jnp.where(at.group == 0, star, 0.0), force)
        out[2 * t] = force[0:4]
        out[2 * t + 1] = force[4:8]
        return carry

    lax.fori_loop(0, (used + LANES - 1) // LANES, run, 0)


def deliver_kernel(rows, cols, partial, out, blocks, from_twin, from_spots, lined, sends, recvs, plane_recv):
    at = Place(rows, cols)
    plane = at.plane
    signal(at.sibling)
    for d in range(1, rows):
        signal({"row": lax.rem(at.row + d, rows)})
    for d in range(1, plane):
        signal(at.at_spot(lax.rem(at.spot + d, plane)))
    blocks[...] = partial[...]
    await_greetings(rows + plane - 1)

    total, left = group_sums(at, blocks, from_twin, from_spots, sends, recvs)
    lined[at.row] = total
    mine = lined.at[at.row]
    for d in range(1, rows):
        remote(mine, mine, sends.at[2], recvs.at[2], {"row": lax.rem(at.row + d, rows)}).start()
    line = lined.at[pl.ds(0, rows - 1)]
    await_bytes(line, recvs.at[2])

    def across(d):
        spot = lax.rem(at.spot + d, plane)
        return remote(lined, out.at[at.core, at.spot], sends.at[3], plane_recv.at[d], at.at_spot(spot))

    for d in range(1, plane):
        across(d).start()
    remote(lined, out.at[at.core, at.spot], sends.at[4], recvs.at[4], at.sibling).start()
    out[at.core, at.spot] = lined[...]
    for d in range(1, plane):
        block = out.at[at.core, lax.rem(at.spot - d + plane, plane)]
        remote(lined, block, sends.at[3], plane_recv.at[d], at.sibling).wait_recv()
        remote(block, block, sends.at[4], recvs.at[4], at.sibling).start()
    await_bytes(out.at[0], recvs.at[4])
    left += [(line, sends.at[2]), (out.at[0], sends.at[4])]
    if plane > 1:
        left.append((out.at[0, pl.ds(0, plane - 1)], sends.at[3]))
    for ref, semaphore in left:
        await_bytes(ref, semaphore)


def finish_kernel(
    rows,
    cols,
    counts,
    forces,
    pos_in,
    vel_in,
    acc_in,
    jerk_in,
    step_in,
    new_pos,
    new_vel,
    new_acc,
    new_jerk,
    total,
    lined,
    pos,
    vel,
    acc,
    jerk,
    step,
    loads,
):
    at = Place(rows, cols)
    pairs = ((pos_in, pos), (vel_in, vel), (acc_in, acc), (jerk_in, jerk), (step_in, step))
    loading = [pltpu.make_async_copy(source, target, loads.at[n]) for n, (source, target) in enumerate(pairs)]
    for load in loading:
        load.start()
    width = pos.shape[1]
    highs = width // LANES
    mine = at.row * cols + at.col
    features = (0, 1, 2, 4, 5, 6)
    share = forces.shape[3]
    together = 8
    at8 = lax.broadcasted_iota(jnp.int32, (highs, LANES), 0)
    at_low = lax.broadcasted_iota(jnp.int32, (LANES, LANES), 0)
    total[...] = jnp.zeros_like(total)

    def one(n, carry):
        t, first = n // (PARTS // together), lax.rem(n, PARTS // together) * together
        lefts, rights = [], []
        for k in range(together):
            member = first + k
            spots = []
            for b in range(2):
                group = (2 * t + b) // share
                z = member // 2 * 2 + group // at.plane
                spots.append((lax.rem(member, 2), lax.rem(group, at.plane), z, lax.rem(2 * t + b, share)))
            star = forces[(*spots[0], slice(3, 4), slice(None))].astype(jnp.int32)
            ok = (star >= 0) & (star // width == mine)
            place = lax.rem(star, width)
            here = jnp.where(ok, place // LANES, -1) == at8
            low = lax.rem(place, LANES)
            rights.append(jnp.where(at_low == low, 1.0, 0.0).astype(BF16))
            pieces = [[], [], []]
            for f in features:
                row = forces[(*spots[f // 4], slice(f % 4, f % 4 + 1), slice(None))]
                for p, piece in enumerate(split3(jnp.where(here, row, 0.0))):
                    pieces[p].append(piece)
            flag = jnp.where(here, 1.0, 0.0)
            blank = jnp.zeros_like(flag)
            lefts.append(jnp.concatenate(pieces[0] + pieces[1] + pieces[2] + [flag, blank], 0).astype(BF16))
        left = jnp.concatenate(lefts, 1)
        right = jnp.concatenate(rights, 1)
        total[...] += lax.dot_general(left, right, (((1,), (1,)), ((), ())), preferred_element_type=F32)
        return carry

    live = lax.fori_loop(0, rows, lambda q, n: n + counts[q, 1, 0], 0)
    lax.fori_loop(0, (live + PARTS - 1) // PARTS * (PARTS // together), one, 0)

    for order in range(7):
        if order < 6:
            parts = [total[(p * 6 + order) * highs : (p * 6 + order + 1) * highs, :] for p in range(3)]
            plane = parts[0] + parts[1] + parts[2]
        else:
            plane = total[18 * highs : 19 * highs, :]
        for c in range(highs):
            lined[order : order + 1, c * LANES : (c + 1) * LANES] = plane[c : c + 1, :]

    for load in loading:
        load.wait()
    on = lined[6:7, :] > 0.5
    a1, k1 = lined[0:3, :], lined[3:6, :]
    x, v, a, k, dt = pos[...], vel[...], acc[...], jerk[...], step[...]
    v1 = v + 0.5 * dt * (a + a1) + dt * dt / 12.0 * (k - k1)
    x1 = x + 0.5 * dt * (v + v1) + dt * dt / 12.0 * (a - a1)
    new_pos[...] = jnp.where(on, x1, x)
    new_vel[...] = jnp.where(on, v1, v)
    new_acc[...] = jnp.where(on, a1, a)
    new_jerk[...] = jnp.where(on, k1, k)


def params(collective_id=None, limit=32 * 2**20):
    if collective_id is None:
        return pltpu.CompilerParams(vmem_limit_bytes=limit)
    return pltpu.CompilerParams(collective_id=collective_id, has_side_effects=True, vmem_limit_bytes=limit)


def per_device(positions, velocities, accels, jerks, masses, elapsed, active, live_tiles):
    rows = lax.axis_size("row")
    cols = lax.axis_size("col")
    width = positions.shape[1]
    tiles = active.shape[0] // TILE
    unit = TILE // PARTS
    blocks = 2 * rows
    plane, layers = cols // 2, rows // 2
    share = blocks // (2 * plane)
    total_stars = width * rows * cols
    dma = pltpu.SemaphoreType.DMA
    triples = [VMEM((3, width), F32) for _ in range(4)]
    single = VMEM((1, width), F32)
    sum_scratch = [
        VMEM((blocks, 4, LANES), F32),
        VMEM((blocks // 2, 4, LANES), F32),
        VMEM((plane, share, 4, LANES), F32),
    ]

    live = jnp.arange(tiles)[:, None] < live_tiles[0]
    named = jnp.where(live, active.reshape(tiles, TILE), -1)
    parts = named.reshape(tiles, PARTS, unit).transpose(1, 0, 2).reshape(PARTS, 1, LANES)
    msg = jnp.concatenate([parts, jnp.broadcast_to(live_tiles[0], parts.shape)], 1)

    ids, states, j_side, j_mass = pl.pallas_call(
        functools.partial(gather_kernel, rows, cols, total_stars),
        out_shape=(
            jax.ShapeDtypeStruct((rows, 2, LANES), jnp.int32),
            jax.ShapeDtypeStruct((blocks, 4, LANES), F32),
            jax.ShapeDtypeStruct((PARTS * width, LANES), BF16),
            jax.ShapeDtypeStruct((32, PARTS * width), BF16),
        ),
        in_specs=[anywhere()] * 6 + [vmem()],
        out_specs=(vmem(),) * 4,
        scratch_shapes=[VMEM((PARTS, 8, width), F32)]
        + sum_scratch
        + [VMEM((6 * PARTS * width // LANES, 3 * LANES), BF16)]
        + triples
        + [single, single, dma((6,)), dma((6,)), dma((4,)), dma, dma]
        + [dma((layers,)), dma((layers,)), dma((2 * layers,))],
        compiler_params=params(0),
        name="gather_states",
    )(positions, velocities, accels, jerks, masses, elapsed, msg)

    pair_count = rows * LANES * PARTS * width
    partial = pl.pallas_call(
        functools.partial(sweep_kernel, rows, cols),
        out_shape=jax.ShapeDtypeStruct((blocks, 4, LANES), F32),
        in_specs=[smem()] + [vmem()] * 4,
        out_specs=vmem(),
        scratch_shapes=[VMEM((rows + 2, 8, LANES), F32)],
        compiler_params=params(),
        cost_estimate=pl.CostEstimate(flops=200 * pair_count, bytes_accessed=2**20, transcendentals=pair_count),
        name="pair_sums",
    )(ids, ids, states, j_side, j_mass)

    forces = pl.pallas_call(
        functools.partial(deliver_kernel, rows, cols),
        out_shape=jax.ShapeDtypeStruct((2, plane, rows, share, 4, LANES), F32),
        in_specs=[vmem()],
        out_specs=vmem(),
        scratch_shapes=sum_scratch + [VMEM((rows, share, 4, LANES), F32), dma((5,)), dma((5,)), dma((plane,))],
        compiler_params=params(1),
        name="deliver_forces",
    )(partial)

    return pl.pallas_call(
        functools.partial(finish_kernel, rows, cols),
        out_shape=tuple(jax.ShapeDtypeStruct((3, width), F32) for _ in range(4)),
        in_specs=[smem(), vmem()] + [anywhere()] * 5,
        out_specs=(vmem(),) * 4,
        scratch_shapes=[VMEM((20 * width // LANES, LANES), F32), VMEM((8, width), F32)] + triples + [single, dma((5,))],
        compiler_params=params(),
        name="finish_step",
    )(ids, forces, positions, velocities, accels, jerks, elapsed)


def solution(mesh):
    stars = P(None, ("row", "col"))
    in_specs = (stars,) * 6 + (P("row"), P("row"))
    return jax.shard_map(per_device, mesh=mesh, in_specs=in_specs, out_specs=(stars,) * 4, check_vma=False)
```

```python
import functools

import jax
import jax.numpy as jnp
from jax import lax
from jax.experimental import pallas as pl
from jax.experimental.pallas import tpu as pltpu
from jax.sharding import PartitionSpec as P

TILE = 128
EPS2 = 0.01
LANES = 128
BLOCK_J = 8192
PIECE_J = 512
PARTS = 16
MESH = pl.DeviceIdType.MESH
VMEM = pltpu.VMEM
F32 = jnp.float32
BF16 = jnp.bfloat16


def vmem():
    return pl.BlockSpec(memory_space=pltpu.VMEM)


def smem():
    return pl.BlockSpec(memory_space=pltpu.SMEM)


def split3(x):
    high = x.astype(BF16).astype(F32)
    rest = x - high
    mid = rest.astype(BF16).astype(F32)
    return high, mid, rest - mid


class Place:
    def __init__(self, rows, cols):
        self.rows, self.cols = rows, cols
        self.side = {32: 4, 8: 2, 2: 1}[cols]
        self.plane, self.layers = self.side * self.side, rows // 2
        self.groups = 2 * self.plane
        self.row = lax.axis_index("row")
        self.col = lax.axis_index("col")
        self.spot, self.core = self.col // 2, lax.rem(self.col, 2)
        self.parity, self.layer = lax.rem(self.row, 2), self.row // 2
        self.group = self.spot * 2 + self.parity
        self.member = self.layer * 2 + self.core
        self.sibling = {"col": self.spot * 2 + 1 - self.core}
        self.twin = {"row": self.layer * 2 + 1 - self.parity}

    def in_layer(self, layer):
        return {"row": layer * 2 + self.parity}

    def at_spot(self, spot):
        return {"col": spot * 2 + self.core}


def signal(device):
    pl.semaphore_signal(pltpu.get_barrier_semaphore(), inc=1, device_id=device, device_id_type=MESH)


def await_greetings(count):
    pl.semaphore_wait(pltpu.get_barrier_semaphore(), count)


def each(first, last, body, step=1):
    def one(n, carry):
        body(first + n * step)
        return carry

    lax.fori_loop(0, (last - first + step - 1) // step, one, 0)


def remote(source, target, send, recv, device):
    return pltpu.make_async_remote_copy(
        src_ref=source, dst_ref=target, send_sem=send, recv_sem=recv, device_id=device, device_id_type=MESH
    )


def await_bytes(ref, semaphore):
    pltpu.make_async_copy(ref, ref, semaphore).wait()


def dots(tile):
    first = lax.broadcasted_iota(jnp.int32, tile.shape, 0) < 3
    swapped = pltpu.roll(tile, 4, 0)
    norm = jnp.sum(jnp.where(first, tile * tile, 0.0), axis=0, keepdims=True)
    cross = jnp.sum(jnp.where(first, tile * swapped, 0.0), axis=0, keepdims=True)
    return norm, cross


def greet(at):
    z_at = lambda d: {"row": lax.rem(at.row + d + at.rows, at.rows)}
    signal(at.sibling)
    for d in (1, -1, 2, -2):
        signal(z_at(d))
    for d in range(1, at.plane):
        signal(at.at_spot(lax.rem(at.spot + d, at.plane)))
    count = 4 + at.plane

    def tell(semaphore, far):
        for d in (far, -far):
            pl.semaphore_signal(semaphore, inc=1, device_id=z_at(d), device_id_type=MESH)

    return count, tell


def plane_sums(at, blocks, from_spots, send, recv, meanwhile):
    span = blocks.shape[0] // at.plane
    from_spots[at.spot] = blocks[pl.ds(at.spot * span, span)]
    left = []
    for d in range(1, at.plane):
        spot = lax.rem(at.spot + d, at.plane)
        part = blocks.at[pl.ds(spot * span, span)]
        remote(part, from_spots.at[at.spot], send, recv, at.at_spot(spot)).start()
    meanwhile()
    if at.plane > 1:
        rest = from_spots.at[pl.ds(0, at.plane - 1)]
        await_bytes(rest, recv)
        left.append((rest, send))
    return jnp.sum(from_spots[...], axis=0), left


def gather_kernel(
    rows,
    cols,
    total_stars,
    x_pred,
    v_pred,
    mass,
    lists,
    live,
    ids,
    states,
    j_side,
    j_mass,
    msg,
    shard,
    picked,
    of_plane,
    from_twin,
    from_spots,
    table,
    sends,
    recvs,
    id_send,
    id_recv,
    right_recv,
    left_recv,
    core_recv,
    four,
    eight,
):
    at = Place(rows, cols)
    me, mine, layers = at.member, at.group, at.layers
    count, tell = greet(at)
    tiles, unit = lists.shape[0], LANES // PARTS
    at_tile = lax.broadcasted_iota(jnp.int32, lists.shape, 0)
    diagonal = lax.broadcasted_iota(jnp.int32, lists.shape, 1) // unit == at_tile
    named = jnp.where(at_tile < live[0], lists[...], -1)
    parts = jnp.zeros_like(named)
    for d in range(tiles):
        turned = jnp.where(diagonal, pltpu.roll(named, unit * d, 1) if d else named, 0)
        parts += pltpu.roll(turned, PARTS - d, 0) if d else turned
    for p in range(PARTS):
        msg[p, 0:1, :] = parts[p : p + 1, :]
        msg[p, 1:2, :] = jnp.full((1, LANES), live[0], jnp.int32)
    ids[at.row] = msg[me]
    shard[me, 0:3, :] = x_pred[...]
    shard[me, 3:4, :] = mass[...] / total_stars
    shard[me, 4:7, :] = v_pred[...]
    shard[me, 7:8, :] = jnp.ones(mass.shape, F32)
    await_greetings(count)
    tell(four, 2)

    width = mass.shape[1]
    chunks = width // LANES

    def prepare(z):
        tile = shard[z]
        norm, cross = dots(tile)
        h, m, l = split3(tile)
        pieces = split3(norm) + split3(cross)
        line = lax.broadcasted_iota(jnp.int32, tile.shape, 0)
        extra = jnp.zeros_like(tile)
        for n, piece in enumerate(pieces):
            extra = jnp.where(line == n, piece, extra)
        blank = jnp.zeros((LANES - 56, width), F32)
        side = jnp.concatenate([h, h, h, m, m, l, extra, blank], 0)
        for c in range(chunks):
            place = pl.ds(pl.multiple_of(z * width + c * LANES, LANES), LANES)
            j_side[place, :] = side[:, c * LANES : (c + 1) * LANES].T.astype(BF16)
        h, m, l = split3(tile * tile[3:4, :])
        place = pl.ds(pl.multiple_of(z * width, width), width)
        j_mass[:, place] = jnp.concatenate([h, m, l, jnp.zeros_like(tile)], 0).astype(BF16)

    def prepare_layers(s, both):
        def one(n):
            layer = lax.rem(at.layer + (n // 2 * 2 - 1) * s + layers, layers)
            prepare(layer * 2 + lax.rem(n, 2))

        each(0, 4 if both else 2, one)

    def ring(s, way, part):
        block = shard.at[lax.rem(at.layer - way * s + layers, layers) * 2 + at.core, :, part]
        recv = (right_recv if way > 0 else left_recv).at[2 * s + (1 if part is halves[1] else 0)]
        return remote(block, block, sends.at[4], recv, at.in_layer(lax.rem(at.layer + way + layers, layers)))

    def arrived(s, way, part):
        block = shard.at[lax.rem(at.layer - way * (s + 1) + 2 * layers, layers) * 2 + at.core, :, part]
        recv = (right_recv if way > 0 else left_recv).at[2 * s + (1 if part is halves[1] else 0)]
        remote(block, block, sends.at[4], recv, at.in_layer(lax.rem(at.layer + way + layers, layers))).wait_recv()

    def across(s, way, core):
        block = shard.at[lax.rem(at.layer - way * s + layers, layers) * 2 + core]
        return remote(block, block, sends.at[5], core_recv.at[2 * s + (1 - way) // 2], at.sibling)

    halves = (pl.ds(0, width // 2), pl.ds(width // 2, width // 2))
    ways = (layers // 2, layers - 1 - layers // 2)
    for s in range(ways[0] + 1):
        for part in halves:
            if s:
                arrived(s - 1, 1, part)
            if 0 < s <= ways[1]:
                arrived(s - 1, -1, part)
            if s < ways[0]:
                ring(s, 1, part).start()
            if s < ways[1]:
                ring(s, -1, part).start()
        across(s, 1, at.core).start()
        if 0 < s <= ways[1]:
            across(s, -1, at.core).start()
        if s == 0:
            pl.semaphore_wait(four, 2)
            tell(eight, 4)
        elif s == 1:
            pl.semaphore_wait(eight, 2)

            def send_ids(d):
                peer = lax.rem(at.row + d, rows)
                part = msg.at[peer // 2 * 2 + at.core]
                remote(part, ids.at[at.row], id_send, id_recv, {"row": peer}).start()

            each(1, rows, send_ids)
        if s:
            across(s - 1, 1, 1 - at.core).wait_recv()
            if 0 < s - 1 <= ways[1]:
                across(s - 1, -1, 1 - at.core).wait_recv()
            if s < ways[0]:
                prepare_layers(s - 1, 0 < s - 1 <= ways[1])
    across(ways[0], 1, 1 - at.core).wait_recv()
    id_rest = ids.at[pl.ds(0, rows - 1)]
    await_bytes(id_rest, id_recv)

    high_count = PARTS * chunks
    features = (0, 1, 2, 4, 5, 6)
    groups = min(4, rows)
    for order, f in enumerate(features):
        plane = jnp.concatenate([shard[:, f, c * LANES : (c + 1) * LANES] for c in range(chunks)], 0)
        h, m, l = split3(plane)
        table[order * high_count : (order + 1) * high_count, :] = jnp.concatenate([h, m, l], 1).astype(BF16)
    picked[...] = jnp.zeros_like(picked)

    def part(g, carry):
        first = g * groups
        star = jnp.concatenate([ids[first + n, 0:1, :] for n in range(groups)], 1)
        owner = star // width
        row, col = owner // cols, lax.rem(owner, cols)
        group = col // 2 * 2 + lax.rem(row, 2)
        member = row // 2 * 2 + lax.rem(col, 2)
        place = lax.rem(star, width)
        high = jnp.where((star >= 0) & (group == mine), place // LANES * PARTS + member, -1)
        low = lax.rem(place, LANES)
        span = groups * LANES
        pick = jnp.where(lax.broadcasted_iota(jnp.int32, (LANES, span), 0) == low, 1.0, 0.0).astype(BF16)
        pick = jnp.concatenate([pick, pick, pick], 0)
        at_row = lax.broadcasted_iota(jnp.int32, (high_count, span), 0) == high
        for order, f in enumerate(features):
            values = jnp.dot(table[order * high_count : (order + 1) * high_count, :], pick, preferred_element_type=F32)
            found = jnp.sum(jnp.where(at_row, values, 0.0), axis=0, keepdims=True)
            for n in range(groups):
                picked[2 * (first + n) + f // 4, f % 4 : f % 4 + 1, :] = found[:, n * LANES : (n + 1) * LANES]
        return carry

    lax.fori_loop(0, rows // groups, part, 0)

    late = ways[0] - 1

    def first_rest():
        prepare_layers(late, 0 < late <= ways[1])

    total, left = plane_sums(at, picked, from_spots, sends.at[0], recvs.at[0], first_rest)
    span = total.shape[0]
    own = pl.ds(at.spot * span, span)
    of_plane[...] = total
    remote(of_plane, from_twin, sends.at[1], recvs.at[1], at.twin).start()
    await_bytes(from_twin, recvs.at[1])
    states[own] = total + from_twin[...]
    for d in range(1, at.plane):
        spot = lax.rem(at.spot + d, at.plane)
        remote(states.at[own], states.at[own], sends.at[2], recvs.at[2], at.at_spot(spot)).start()
    prepare_layers(ways[0], False)
    if at.plane > 1:
        rest = states.at[pl.ds(0, states.shape[0] - span)]
        await_bytes(rest, recvs.at[2])
        left.append((rest, sends.at[2]))
    left += [
        (of_plane, sends.at[1]),
        (shard.at[pl.ds(0, layers - 1)], sends.at[4]),
        (shard.at[pl.ds(0, layers)], sends.at[5]),
        (id_rest, id_send),
    ]
    for ref, semaphore in left:
        await_bytes(ref, semaphore)


def sweep_kernel(rows, cols, counts, ids, states, j_side, j_mass, out, i_tiles):
    at = Place(rows, cols)
    total = j_side.shape[0]
    at8 = lax.broadcasted_iota(jnp.int32, (8, LANES), 0)
    lane = lax.broadcasted_iota(jnp.int32, (8, LANES), 1)
    out[...] = jnp.zeros_like(out)
    i_tiles[...] = jnp.where(lax.broadcasted_iota(jnp.int32, i_tiles.shape, 1) == 3, -1.0, 0.0)

    def pack(q, offset):
        tile = jnp.concatenate([states[2 * q], states[2 * q + 1]], 0)
        tile = jnp.where(at8 == 3, ids[q, 0:1, :].astype(F32), tile)
        t, shift = offset // LANES, lax.rem(offset, LANES)
        rolled = pltpu.roll(tile, shift, 1)
        i_tiles[t] = jnp.where(lane >= shift, rolled, i_tiles[t])
        i_tiles[t + 1] = jnp.where(lane < shift, rolled, i_tiles[t + 1])
        return offset + counts[q, 1, 0] * (TILE // PARTS)

    used = lax.fori_loop(0, rows, pack, 0)

    def right_of(tile):
        norm, cross = dots(tile)
        h, m, l = split3(tile)
        nh, nm, nl = split3(norm + EPS2)
        ch, cm, cl = split3(cross)

        def for_r(piece, last):
            return jnp.where(at8 < 3, -2.0 * piece, jnp.where(at8 == 7, last, 0.0))

        def for_b(piece, last):
            return jnp.where(at8 == 7, last, jnp.where(at8 == 3, 0.0, -pltpu.roll(piece, 4, 0)))

        r_extra = jnp.where(at8 < 3, 1.0, 0.0)
        b_extra = jnp.where((at8 >= 3) & (at8 < 6), 1.0, 0.0)
        blank = jnp.zeros((LANES - 56, LANES), F32)
        right_r = jnp.concatenate(
            [for_r(h, nh), for_r(m, nm), for_r(l, nl), for_r(h, 0.0), for_r(m, 0.0), for_r(h, 0.0), r_extra, blank], 0
        )
        right_b = jnp.concatenate(
            [for_b(h, ch), for_b(m, cm), for_b(l, cl), for_b(h, 0.0), for_b(m, 0.0), for_b(h, 0.0), b_extra, blank], 0
        )
        return jnp.concatenate([right_r, right_b], 1).astype(BF16)

    def run(t, carry):
        tile = i_tiles[t]
        right = right_of(tile)

        def one_block(n, sums):
            def place(s):
                return pl.ds(pl.multiple_of(n * BLOCK_J + s * PIECE_J, PIECE_J), PIECE_J)

            def distances(s):
                return jnp.dot(j_side[place(s), :], right, preferred_element_type=F32)

            ahead = distances(0)
            for s in range(BLOCK_J // PIECE_J):
                both = ahead
                if s + 1 < BLOCK_J // PIECE_J:
                    ahead = distances(s + 1)
                inverse = lax.rsqrt(both[:, 0:LANES])
                square = inverse * inverse
                near = square * inverse
                tilt = near * square * both[:, LANES:]
                pair = jnp.concatenate([near, tilt], 1)
                high = pair.astype(BF16)
                low = (pair - high.astype(F32)).astype(BF16)
                weights = j_mass[:, place(s)]
                sums += jnp.dot(
                    jnp.concatenate([weights, weights], 1),
                    jnp.concatenate([high, low], 0),
                    preferred_element_type=F32,
                )
            return sums

        sums = lax.fori_loop(0, total // BLOCK_J, one_block, jnp.zeros((32, 2 * LANES), F32))
        sums = sums[0:8] + sums[8:16] + sums[16:24]
        near, tilt = sums[:, 0:LANES], sums[:, LANES:]
        near = near - tile * near[7:8]
        tilt = tilt - tile * tilt[7:8]
        force = near - jnp.where(at8 >= 4, 3.0 * pltpu.roll(tilt, 4, 0), 0.0)
        star = tile[3:4]
        force = jnp.where(star >= 0, force, 0.0)
        force = jnp.where(at8 == 3, jnp.where(at.group == 0, star, 0.0), force)
        out[2 * t] = force[0:4]
        out[2 * t + 1] = force[4:8]
        return carry

    lax.fori_loop(0, (used + LANES - 1) // LANES, run, 0)


def deliver_kernel(rows, cols, blocks, out, of_plane, from_twin, from_spots, lined, sends, recvs, plane_recv, four, eight):
    at = Place(rows, cols)
    plane = at.plane
    count, tell = greet(at)
    await_greetings(count)
    tell(four, 2)

    def wider():
        pl.semaphore_wait(four, 2)
        tell(eight, 4)

    total, left = plane_sums(at, blocks, from_spots, sends.at[0], recvs.at[0], wider)
    share = total.shape[0] // 2
    of_plane[...] = total
    theirs = of_plane.at[pl.ds((1 - at.parity) * share, share)]
    from_there = from_twin.at[pl.ds(0, share)]
    remote(theirs, from_there, sends.at[5], recvs.at[5], at.twin).start()
    left.append((theirs, sends.at[5]))
    pl.semaphore_wait(eight, 2)
    await_bytes(from_there, recvs.at[5])
    lined[at.row] = of_plane[pl.ds(at.parity * share, share)] + from_there[...]
    mine = lined.at[at.row]
    for d in range(1, rows):
        remote(mine, mine, sends.at[2], recvs.at[2], {"row": lax.rem(at.row + d, rows)}).start()
    line = lined.at[pl.ds(0, rows - 1)]
    await_bytes(line, recvs.at[2])

    def across(d):
        spot = lax.rem(at.spot + d, plane)
        return remote(lined, out.at[at.core, at.spot], sends.at[3], plane_recv.at[d], at.at_spot(spot))

    for d in range(1, plane):
        across(d).start()
    remote(lined, out.at[at.core, at.spot], sends.at[4], recvs.at[4], at.sibling).start()
    out[at.core, at.spot] = lined[...]
    for d in range(1, plane):
        block = out.at[at.core, lax.rem(at.spot - d + plane, plane)]
        remote(lined, block, sends.at[3], plane_recv.at[d], at.sibling).wait_recv()
        remote(block, block, sends.at[4], recvs.at[4], at.sibling).start()
    await_bytes(out.at[0], recvs.at[4])
    left += [(line, sends.at[2]), (out.at[0], sends.at[4])]
    if plane > 1:
        left.append((out.at[0, pl.ds(0, plane - 1)], sends.at[3]))
    for ref, semaphore in left:
        await_bytes(ref, semaphore)


def finish_kernel(
    rows, cols, counts, forces, pos, vel, acc, jerk, step, new_pos, new_vel, new_acc, new_jerk, total, lined
):
    at = Place(rows, cols)
    width = pos.shape[1]
    highs = width // LANES
    mine = at.row * cols + at.col
    features = (0, 1, 2, 4, 5, 6)
    share = forces.shape[3]
    together = 16
    at8 = lax.broadcasted_iota(jnp.int32, (highs, LANES), 0)
    at_low = lax.broadcasted_iota(jnp.int32, (LANES, LANES), 0)
    total[...] = jnp.zeros_like(total)

    def one(n, carry):
        t, first = n // (PARTS // together), lax.rem(n, PARTS // together) * together
        lefts, rights = [], []
        for k in range(together):
            member = first + k
            spots = []
            for b in range(2):
                group = (2 * t + b) // share
                z = member // 2 * 2 + lax.rem(group, 2)
                spots.append((lax.rem(member, 2), group // 2, z, lax.rem(2 * t + b, share)))
            star = forces[(*spots[0], slice(3, 4), slice(None))].astype(jnp.int32)
            ok = (star >= 0) & (star // width == mine)
            place = lax.rem(star, width)
            here = jnp.where(ok, place // LANES, -1) == at8
            low = lax.rem(place, LANES)
            rights.append(jnp.where(at_low == low, 1.0, 0.0).astype(BF16))
            pieces = [[], [], []]
            for f in features:
                row = forces[(*spots[f // 4], slice(f % 4, f % 4 + 1), slice(None))]
                for p, piece in enumerate(split3(jnp.where(here, row, 0.0))):
                    pieces[p].append(piece)
            flag = jnp.where(here, 1.0, 0.0)
            blank = jnp.zeros_like(flag)
            lefts.append(jnp.concatenate(pieces[0] + pieces[1] + pieces[2] + [flag, blank], 0).astype(BF16))
        left = jnp.concatenate(lefts, 1)
        right = jnp.concatenate(rights, 1)
        total[...] += lax.dot_general(left, right, (((1,), (1,)), ((), ())), preferred_element_type=F32)
        return carry

    live = lax.fori_loop(0, rows, lambda q, n: n + counts[q, 1, 0], 0)
    lax.fori_loop(0, (live + PARTS - 1) // PARTS * (PARTS // together), one, 0)

    for order in range(7):
        if order < 6:
            parts = [total[(p * 6 + order) * highs : (p * 6 + order + 1) * highs, :] for p in range(3)]
            plane = parts[0] + parts[1] + parts[2]
        else:
            plane = total[18 * highs : 19 * highs, :]
        for c in range(highs):
            lined[order : order + 1, c * LANES : (c + 1) * LANES] = plane[c : c + 1, :]

    on = lined[6:7, :] > 0.5
    a1, k1 = lined[0:3, :], lined[3:6, :]
    x, v, a, k, dt = pos[...], vel[...], acc[...], jerk[...], step[...]
    v1 = v + 0.5 * dt * (a + a1) + dt * dt / 12.0 * (k - k1)
    x1 = x + 0.5 * dt * (v + v1) + dt * dt / 12.0 * (a - a1)
    new_pos[...] = jnp.where(on, x1, x)
    new_vel[...] = jnp.where(on, v1, v)
    new_acc[...] = jnp.where(on, a1, a)
    new_jerk[...] = jnp.where(on, k1, k)


def params(collective_id=None, limit=32 * 2**20):
    if collective_id is None:
        return pltpu.CompilerParams(vmem_limit_bytes=limit)
    return pltpu.CompilerParams(collective_id=collective_id, has_side_effects=True, vmem_limit_bytes=limit)


def per_device(positions, velocities, accels, jerks, masses, elapsed, active, live_tiles):
    rows = lax.axis_size("row")
    cols = lax.axis_size("col")
    width = positions.shape[1]
    blocks = 2 * rows
    plane, layers = cols // 2, rows // 2
    share = blocks // (2 * plane)
    total_stars = width * rows * cols
    dma, told = pltpu.SemaphoreType.DMA, pltpu.SemaphoreType.REGULAR
    sum_scratch = [VMEM((2 * share, 4, LANES), F32)] * 2 + [VMEM((plane, 2 * share, 4, LANES), F32)]

    x_pred = positions + elapsed * (velocities + elapsed * (0.5 * accels + elapsed * jerks / 6.0))
    v_pred = velocities + elapsed * (accels + elapsed * jerks / 2.0)
    ids, states, j_side, j_mass = pl.pallas_call(
        functools.partial(gather_kernel, rows, cols, total_stars),
        out_shape=(
            jax.ShapeDtypeStruct((rows, 2, LANES), jnp.int32),
            jax.ShapeDtypeStruct((blocks, 4, LANES), F32),
            jax.ShapeDtypeStruct((PARTS * width, LANES), BF16),
            jax.ShapeDtypeStruct((32, PARTS * width), BF16),
        ),
        in_specs=[vmem()] * 4 + [smem()],
        out_specs=(vmem(),) * 4,
        scratch_shapes=[VMEM((PARTS, 2, LANES), jnp.int32), VMEM((PARTS, 8, width), F32), VMEM((blocks, 4, LANES), F32)]
        + sum_scratch
        + [VMEM((6 * PARTS * width // LANES, 3 * LANES), BF16)]
        + [dma((6,)), dma((4,)), dma, dma]
        + [dma((2 * layers,)) for _ in range(3)]
        + [told, told],
        compiler_params=params(0),
        name="gather_states",
    )(x_pred, v_pred, masses, active.reshape(active.shape[0] // TILE, TILE), live_tiles)

    pair_count = rows * LANES * PARTS * width
    partial = pl.pallas_call(
        functools.partial(sweep_kernel, rows, cols),
        out_shape=jax.ShapeDtypeStruct((blocks, 4, LANES), F32),
        in_specs=[smem()] + [vmem()] * 4,
        out_specs=vmem(),
        scratch_shapes=[VMEM((rows + 2, 8, LANES), F32)],
        compiler_params=params(),
        cost_estimate=pl.CostEstimate(flops=200 * pair_count, bytes_accessed=2**20, transcendentals=pair_count),
        name="pair_sums",
    )(ids, ids, states, j_side, j_mass)

    forces = pl.pallas_call(
        functools.partial(deliver_kernel, rows, cols),
        out_shape=jax.ShapeDtypeStruct((2, plane, rows, share, 4, LANES), F32),
        in_specs=[vmem()],
        out_specs=vmem(),
        scratch_shapes=sum_scratch + [VMEM((rows, share, 4, LANES), F32), dma((6,)), dma((6,)), dma((plane,)), told, told],
        compiler_params=params(1),
        name="deliver_forces",
    )(partial)

    return pl.pallas_call(
        functools.partial(finish_kernel, rows, cols),
        out_shape=tuple(jax.ShapeDtypeStruct((3, width), F32) for _ in range(4)),
        in_specs=[smem()] + [vmem()] * 6,
        out_specs=(vmem(),) * 4,
        scratch_shapes=[VMEM((20 * width // LANES, LANES), F32), VMEM((8, width), F32)],
        compiler_params=params(),
        name="finish_step",
    )(ids, forces, positions, velocities, accels, jerks, elapsed)


def solution(mesh):
    stars = P(None, ("row", "col"))
    in_specs = (stars,) * 6 + (P("row"), P("row"))
    return jax.shard_map(per_device, mesh=mesh, in_specs=in_specs, out_specs=(stars,) * 4, check_vma=False)
```

```python
import functools

import jax
import jax.numpy as jnp
from jax import lax
from jax.experimental import pallas as pl
from jax.experimental.pallas import tpu as pltpu
from jax.sharding import PartitionSpec as P

TILE = 128
EPS2 = 0.01
LANES = 128
BLOCK_J = 16384
PIECE_J = 512
PARTS = 16
MESH = pl.DeviceIdType.MESH
VMEM = pltpu.VMEM
F32 = jnp.float32
BF16 = jnp.bfloat16


def vmem():
    return pl.BlockSpec(memory_space=pltpu.VMEM)


def smem():
    return pl.BlockSpec(memory_space=pltpu.SMEM)


def split3(x):
    high = x.astype(BF16).astype(F32)
    rest = x - high
    mid = rest.astype(BF16).astype(F32)
    return high, mid, rest - mid


class Place:
    def __init__(self, rows, cols):
        self.rows, self.cols = rows, cols
        self.side = {32: 4, 8: 2, 2: 1}[cols]
        self.plane, self.layers = self.side * self.side, rows // 2
        self.groups = 2 * self.plane
        self.row = lax.axis_index("row")
        self.col = lax.axis_index("col")
        self.spot, self.core = self.col // 2, lax.rem(self.col, 2)
        self.parity, self.layer = lax.rem(self.row, 2), self.row // 2
        self.group = self.spot * 2 + self.parity
        self.member = self.layer * 2 + self.core
        self.sibling = {"col": self.spot * 2 + 1 - self.core}
        self.twin = {"row": self.layer * 2 + 1 - self.parity}

    def in_layer(self, layer):
        return {"row": layer * 2 + self.parity}

    def at_spot(self, spot):
        return {"col": spot * 2 + self.core}


def signal(device):
    pl.semaphore_signal(pltpu.get_barrier_semaphore(), inc=1, device_id=device, device_id_type=MESH)


def await_greetings(count):
    pl.semaphore_wait(pltpu.get_barrier_semaphore(), count)


def each(first, last, body, step=1):
    def one(n, carry):
        body(first + n * step)
        return carry

    lax.fori_loop(0, (last - first + step - 1) // step, one, 0)


def remote(source, target, send, recv, device):
    return pltpu.make_async_remote_copy(
        src_ref=source, dst_ref=target, send_sem=send, recv_sem=recv, device_id=device, device_id_type=MESH
    )


def await_bytes(ref, semaphore):
    pltpu.make_async_copy(ref, ref, semaphore).wait()


def dots(tile):
    first = lax.broadcasted_iota(jnp.int32, tile.shape, 0) < 3
    swapped = pltpu.roll(tile, 4, 0)
    norm = jnp.sum(jnp.where(first, tile * tile, 0.0), axis=0, keepdims=True)
    cross = jnp.sum(jnp.where(first, tile * swapped, 0.0), axis=0, keepdims=True)
    return norm, cross


def greet(at):
    z_at = lambda d: {"row": lax.rem(at.row + d + at.rows, at.rows)}
    signal(at.sibling)
    for d in (1, -1, 2, -2):
        signal(z_at(d))
    for d in range(1, at.plane):
        signal(at.at_spot(lax.rem(at.spot + d, at.plane)))
    count = 4 + at.plane

    def tell(semaphore, far):
        for d in (far, -far):
            pl.semaphore_signal(semaphore, inc=1, device_id=z_at(d), device_id_type=MESH)

    return count, tell


def plane_sums(at, blocks, from_spots, send, recv, meanwhile):
    span = blocks.shape[0] // at.plane
    from_spots[at.spot] = blocks[pl.ds(at.spot * span, span)]
    left = []
    for d in range(1, at.plane):
        spot = lax.rem(at.spot + d, at.plane)
        part = blocks.at[pl.ds(spot * span, span)]
        remote(part, from_spots.at[at.spot], send, recv, at.at_spot(spot)).start()
    meanwhile()
    if at.plane > 1:
        rest = from_spots.at[pl.ds(0, at.plane - 1)]
        await_bytes(rest, recv)
        left.append((rest, send))
    return jnp.sum(from_spots[...], axis=0), left


def gather_kernel(
    rows,
    cols,
    total_stars,
    x_pred,
    v_pred,
    mass,
    lists,
    live,
    ids,
    states,
    j_side,
    j_mass,
    msg,
    shard,
    picked,
    of_plane,
    from_twin,
    from_spots,
    table,
    sends,
    recvs,
    id_send,
    id_recv,
    right_recv,
    left_recv,
    core_recv,
    four,
    eight,
):
    at = Place(rows, cols)
    me, mine, layers = at.member, at.group, at.layers
    count, tell = greet(at)
    tiles, unit = lists.shape[0], LANES // PARTS
    at_tile = lax.broadcasted_iota(jnp.int32, lists.shape, 0)
    diagonal = lax.broadcasted_iota(jnp.int32, lists.shape, 1) // unit == at_tile
    named = jnp.where(at_tile < live[0], lists[...], -1)
    parts = jnp.zeros_like(named)
    for d in range(tiles):
        turned = jnp.where(diagonal, pltpu.roll(named, unit * d, 1) if d else named, 0)
        parts += pltpu.roll(turned, PARTS - d, 0) if d else turned
    for p in range(PARTS):
        msg[p, 0:1, :] = parts[p : p + 1, :]
        msg[p, 1:2, :] = jnp.full((1, LANES), live[0], jnp.int32)
    ids[at.row] = msg[me]
    shard[me, 0:3, :] = x_pred[...]
    shard[me, 3:4, :] = mass[...] / total_stars
    shard[me, 4:7, :] = v_pred[...]
    shard[me, 7:8, :] = jnp.ones(mass.shape, F32)
    await_greetings(count)
    tell(four, 2)

    width = mass.shape[1]
    chunks = width // LANES

    def prepare(z):
        tile = shard[z]
        norm, cross = dots(tile)
        h, m, l = split3(tile)
        pieces = split3(norm) + split3(cross)
        line = lax.broadcasted_iota(jnp.int32, tile.shape, 0)
        extra = jnp.zeros_like(tile)
        for n, piece in enumerate(pieces):
            extra = jnp.where(line == n, piece, extra)
        blank = jnp.zeros((LANES - 56, width), F32)
        side = jnp.concatenate([h, h, h, m, m, l, extra, blank], 0)
        for c in range(chunks):
            place = pl.ds(pl.multiple_of(z * width + c * LANES, LANES), LANES)
            j_side[place, :] = side[:, c * LANES : (c + 1) * LANES].T.astype(BF16)
        h, m, l = split3(tile * tile[3:4, :])
        place = pl.ds(pl.multiple_of(z * width, width), width)
        j_mass[:, place] = jnp.concatenate([h, m, l, jnp.zeros_like(tile)], 0).astype(BF16)

    def prepare_layers(s, both):
        def one(n):
            layer = lax.rem(at.layer + (n // 2 * 2 - 1) * s + layers, layers)
            prepare(layer * 2 + lax.rem(n, 2))

        each(0, 4 if both else 2, one)

    def ring(s, way, part):
        block = shard.at[lax.rem(at.layer - way * s + layers, layers) * 2 + at.core, :, part]
        recv = (right_recv if way > 0 else left_recv).at[2 * s + (1 if part is halves[1] else 0)]
        return remote(block, block, sends.at[4], recv, at.in_layer(lax.rem(at.layer + way + layers, layers)))

    def arrived(s, way, part):
        block = shard.at[lax.rem(at.layer - way * (s + 1) + 2 * layers, layers) * 2 + at.core, :, part]
        recv = (right_recv if way > 0 else left_recv).at[2 * s + (1 if part is halves[1] else 0)]
        remote(block, block, sends.at[4], recv, at.in_layer(lax.rem(at.layer + way + layers, layers))).wait_recv()

    def across(s, way, core):
        block = shard.at[lax.rem(at.layer - way * s + layers, layers) * 2 + core]
        return remote(block, block, sends.at[5], core_recv.at[2 * s + (1 - way) // 2], at.sibling)

    halves = (pl.ds(0, width // 2), pl.ds(width // 2, width // 2))
    ways = (layers // 2, layers - 1 - layers // 2)
    for s in range(ways[0] + 1):
        for part in halves:
            if s:
                arrived(s - 1, 1, part)
            if 0 < s <= ways[1]:
                arrived(s - 1, -1, part)
            if s < ways[0]:
                ring(s, 1, part).start()
            if s < ways[1]:
                ring(s, -1, part).start()
        across(s, 1, at.core).start()
        if 0 < s <= ways[1]:
            across(s, -1, at.core).start()
        if s == 0:
            pl.semaphore_wait(four, 2)
            tell(eight, 4)
        elif s == 1:
            pl.semaphore_wait(eight, 2)

            def send_ids(d):
                peer = lax.rem(at.row + d, rows)
                part = msg.at[peer // 2 * 2 + at.core]
                remote(part, ids.at[at.row], id_send, id_recv, {"row": peer}).start()

            each(1, rows, send_ids)
        if s:
            across(s - 1, 1, 1 - at.core).wait_recv()
            if 0 < s - 1 <= ways[1]:
                across(s - 1, -1, 1 - at.core).wait_recv()
            if s < ways[0]:
                prepare_layers(s - 1, 0 < s - 1 <= ways[1])
    across(ways[0], 1, 1 - at.core).wait_recv()
    id_rest = ids.at[pl.ds(0, rows - 1)]
    await_bytes(id_rest, id_recv)

    high_count = PARTS * chunks
    features = (0, 1, 2, 4, 5, 6)
    groups = min(8, rows)
    for order, f in enumerate(features):
        plane = jnp.concatenate([shard[:, f, c * LANES : (c + 1) * LANES] for c in range(chunks)], 0)
        h, m, l = split3(plane)
        table[order * high_count : (order + 1) * high_count, :] = jnp.concatenate([h, m, l], 1).astype(BF16)
    picked[...] = jnp.zeros_like(picked)

    def part(g, carry):
        first = g * groups
        star = jnp.concatenate([ids[first + n, 0:1, :] for n in range(groups)], 1)
        owner = star // width
        row, col = owner // cols, lax.rem(owner, cols)
        group = col // 2 * 2 + lax.rem(row, 2)
        member = row // 2 * 2 + lax.rem(col, 2)
        place = lax.rem(star, width)
        high = jnp.where((star >= 0) & (group == mine), place // LANES * PARTS + member, -1)
        low = lax.rem(place, LANES)
        span = groups * LANES
        pick = jnp.where(lax.broadcasted_iota(jnp.int32, (LANES, span), 0) == low, 1.0, 0.0).astype(BF16)
        pick = jnp.concatenate([pick, pick, pick], 0)
        at_row = lax.broadcasted_iota(jnp.int32, (high_count, span), 0) == high
        for order, f in enumerate(features):
            values = jnp.dot(table[order * high_count : (order + 1) * high_count, :], pick, preferred_element_type=F32)
            found = jnp.sum(jnp.where(at_row, values, 0.0), axis=0, keepdims=True)
            for n in range(groups):
                picked[2 * (first + n) + f // 4, f % 4 : f % 4 + 1, :] = found[:, n * LANES : (n + 1) * LANES]
        return carry

    lax.fori_loop(0, rows // groups, part, 0)

    late = ways[0] - 1

    def first_rest():
        prepare_layers(late, 0 < late <= ways[1])

    total, left = plane_sums(at, picked, from_spots, sends.at[0], recvs.at[0], first_rest)
    span = total.shape[0]
    own = pl.ds(at.spot * span, span)
    of_plane[...] = total
    remote(of_plane, from_twin, sends.at[1], recvs.at[1], at.twin).start()
    await_bytes(from_twin, recvs.at[1])
    states[own] = total + from_twin[...]
    for d in range(1, at.plane):
        spot = lax.rem(at.spot + d, at.plane)
        remote(states.at[own], states.at[own], sends.at[2], recvs.at[2], at.at_spot(spot)).start()
    prepare_layers(ways[0], False)
    if at.plane > 1:
        rest = states.at[pl.ds(0, states.shape[0] - span)]
        await_bytes(rest, recvs.at[2])
        left.append((rest, sends.at[2]))
    left += [
        (of_plane, sends.at[1]),
        (shard.at[pl.ds(0, layers - 1)], sends.at[4]),
        (shard.at[pl.ds(0, layers)], sends.at[5]),
        (id_rest, id_send),
    ]
    for ref, semaphore in left:
        await_bytes(ref, semaphore)


def sweep_kernel(rows, cols, counts, ids, states, j_side, j_mass, out, i_tiles):
    at = Place(rows, cols)
    total = j_side.shape[0]
    at8 = lax.broadcasted_iota(jnp.int32, (8, LANES), 0)
    lane = lax.broadcasted_iota(jnp.int32, (8, LANES), 1)
    out[...] = jnp.zeros_like(out)
    i_tiles[...] = jnp.where(lax.broadcasted_iota(jnp.int32, i_tiles.shape, 1) == 3, -1.0, 0.0)

    def pack(q, offset):
        tile = jnp.concatenate([states[2 * q], states[2 * q + 1]], 0)
        tile = jnp.where(at8 == 3, ids[q, 0:1, :].astype(F32), tile)
        t, shift = offset // LANES, lax.rem(offset, LANES)
        rolled = pltpu.roll(tile, shift, 1)
        i_tiles[t] = jnp.where(lane >= shift, rolled, i_tiles[t])
        i_tiles[t + 1] = jnp.where(lane < shift, rolled, i_tiles[t + 1])
        return offset + counts[q, 1, 0] * (TILE // PARTS)

    used = lax.fori_loop(0, rows, pack, 0)

    def right_of(tile):
        norm, cross = dots(tile)
        h, m, l = split3(tile)
        nh, nm, nl = split3(norm + EPS2)
        ch, cm, cl = split3(cross)

        def for_r(piece, last):
            return jnp.where(at8 < 3, -2.0 * piece, jnp.where(at8 == 7, last, 0.0))

        def for_b(piece, last):
            return jnp.where(at8 == 7, last, jnp.where(at8 == 3, 0.0, -pltpu.roll(piece, 4, 0)))

        r_extra = jnp.where(at8 < 3, 1.0, 0.0)
        b_extra = jnp.where((at8 >= 3) & (at8 < 6), 1.0, 0.0)
        blank = jnp.zeros((LANES - 56, LANES), F32)
        right_r = jnp.concatenate(
            [for_r(h, nh), for_r(m, nm), for_r(l, nl), for_r(h, 0.0), for_r(m, 0.0), for_r(h, 0.0), r_extra, blank], 0
        )
        right_b = jnp.concatenate(
            [for_b(h, ch), for_b(m, cm), for_b(l, cl), for_b(h, 0.0), for_b(m, 0.0), for_b(h, 0.0), b_extra, blank], 0
        )
        return jnp.concatenate([right_r, right_b], 1).astype(BF16)

    def run(t, carry):
        tile = i_tiles[t]
        right = right_of(tile)

        def one_block(n, sums):
            def place(s):
                return pl.ds(pl.multiple_of(n * BLOCK_J + s * PIECE_J, PIECE_J), PIECE_J)

            def distances(s):
                return jnp.dot(j_side[place(s), :], right, preferred_element_type=F32)

            ahead = distances(0)
            for s in range(BLOCK_J // PIECE_J):
                both = ahead
                if s + 1 < BLOCK_J // PIECE_J:
                    ahead = distances(s + 1)
                inverse = lax.rsqrt(both[:, 0:LANES])
                square = inverse * inverse
                near = square * inverse
                tilt = near * square * both[:, LANES:]
                pair = jnp.concatenate([near, tilt], 1)
                high = pair.astype(BF16)
                low = (pair - high.astype(F32)).astype(BF16)
                weights = j_mass[:, place(s)]
                sums += jnp.dot(
                    jnp.concatenate([weights, weights], 1),
                    jnp.concatenate([high, low], 0),
                    preferred_element_type=F32,
                )
            return sums

        sums = lax.fori_loop(0, total // BLOCK_J, one_block, jnp.zeros((32, 2 * LANES), F32))
        sums = sums[0:8] + sums[8:16] + sums[16:24]
        near, tilt = sums[:, 0:LANES], sums[:, LANES:]
        near = near - tile * near[7:8]
        tilt = tilt - tile * tilt[7:8]
        force = near - jnp.where(at8 >= 4, 3.0 * pltpu.roll(tilt, 4, 0), 0.0)
        star = tile[3:4]
        force = jnp.where(star >= 0, force, 0.0)
        force = jnp.where(at8 == 3, jnp.where(at.group == 0, star, 0.0), force)
        out[2 * t] = force[0:4]
        out[2 * t + 1] = force[4:8]
        return carry

    lax.fori_loop(0, (used + LANES - 1) // LANES, run, 0)


def deliver_kernel(rows, cols, blocks, out, of_plane, from_twin, from_spots, lined, sends, recvs, plane_recv, four, eight):
    at = Place(rows, cols)
    plane = at.plane
    count, tell = greet(at)
    await_greetings(count)
    tell(four, 2)

    def wider():
        pl.semaphore_wait(four, 2)
        tell(eight, 4)

    total, left = plane_sums(at, blocks, from_spots, sends.at[0], recvs.at[0], wider)
    share = total.shape[0] // 2
    of_plane[...] = total
    theirs = of_plane.at[pl.ds((1 - at.parity) * share, share)]
    from_there = from_twin.at[pl.ds(0, share)]
    remote(theirs, from_there, sends.at[5], recvs.at[5], at.twin).start()
    left.append((theirs, sends.at[5]))
    pl.semaphore_wait(eight, 2)
    await_bytes(from_there, recvs.at[5])
    lined[at.row] = of_plane[pl.ds(at.parity * share, share)] + from_there[...]
    mine = lined.at[at.row]
    for d in range(1, rows):
        remote(mine, mine, sends.at[2], recvs.at[2], {"row": lax.rem(at.row + d, rows)}).start()
    line = lined.at[pl.ds(0, rows - 1)]
    await_bytes(line, recvs.at[2])

    def across(d):
        spot = lax.rem(at.spot + d, plane)
        return remote(lined, out.at[at.core, at.spot], sends.at[3], plane_recv.at[d], at.at_spot(spot))

    for d in range(1, plane):
        across(d).start()
    remote(lined, out.at[at.core, at.spot], sends.at[4], recvs.at[4], at.sibling).start()
    out[at.core, at.spot] = lined[...]
    for d in range(1, plane):
        block = out.at[at.core, lax.rem(at.spot - d + plane, plane)]
        remote(lined, block, sends.at[3], plane_recv.at[d], at.sibling).wait_recv()
        remote(block, block, sends.at[4], recvs.at[4], at.sibling).start()
    await_bytes(out.at[0], recvs.at[4])
    left += [(line, sends.at[2]), (out.at[0], sends.at[4])]
    if plane > 1:
        left.append((out.at[0, pl.ds(0, plane - 1)], sends.at[3]))
    for ref, semaphore in left:
        await_bytes(ref, semaphore)


def finish_kernel(
    rows, cols, counts, forces, pos, vel, acc, jerk, step, new_pos, new_vel, new_acc, new_jerk, total, lined
):
    at = Place(rows, cols)
    width = pos.shape[1]
    highs = width // LANES
    mine = at.row * cols + at.col
    features = (0, 1, 2, 4, 5, 6)
    share = forces.shape[3]
    together = 16
    at8 = lax.broadcasted_iota(jnp.int32, (highs, LANES), 0)
    at_low = lax.broadcasted_iota(jnp.int32, (LANES, LANES), 0)
    total[...] = jnp.zeros_like(total)

    def one(n, carry):
        t, first = n // (PARTS // together), lax.rem(n, PARTS // together) * together
        lefts, rights = [], []
        for k in range(together):
            member = first + k
            spots = []
            for b in range(2):
                group = (2 * t + b) // share
                z = member // 2 * 2 + lax.rem(group, 2)
                spots.append((lax.rem(member, 2), group // 2, z, lax.rem(2 * t + b, share)))
            star = forces[(*spots[0], slice(3, 4), slice(None))].astype(jnp.int32)
            ok = (star >= 0) & (star // width == mine)
            place = lax.rem(star, width)
            here = jnp.where(ok, place // LANES, -1) == at8
            low = lax.rem(place, LANES)
            rights.append(jnp.where(at_low == low, 1.0, 0.0).astype(BF16))
            pieces = [[], [], []]
            for f in features:
                row = forces[(*spots[f // 4], slice(f % 4, f % 4 + 1), slice(None))]
                for p, piece in enumerate(split3(jnp.where(here, row, 0.0))):
                    pieces[p].append(piece)
            flag = jnp.where(here, 1.0, 0.0)
            blank = jnp.zeros_like(flag)
            lefts.append(jnp.concatenate(pieces[0] + pieces[1] + pieces[2] + [flag, blank], 0).astype(BF16))
        left = jnp.concatenate(lefts, 1)
        right = jnp.concatenate(rights, 1)
        total[...] += lax.dot_general(left, right, (((1,), (1,)), ((), ())), preferred_element_type=F32)
        return carry

    live = lax.fori_loop(0, rows, lambda q, n: n + counts[q, 1, 0], 0)
    lax.fori_loop(0, (live + PARTS - 1) // PARTS * (PARTS // together), one, 0)

    for order in range(7):
        if order < 6:
            parts = [total[(p * 6 + order) * highs : (p * 6 + order + 1) * highs, :] for p in range(3)]
            plane = parts[0] + parts[1] + parts[2]
        else:
            plane = total[18 * highs : 19 * highs, :]
        for c in range(highs):
            lined[order : order + 1, c * LANES : (c + 1) * LANES] = plane[c : c + 1, :]

    on = lined[6:7, :] > 0.5
    a1, k1 = lined[0:3, :], lined[3:6, :]
    x, v, a, k, dt = pos[...], vel[...], acc[...], jerk[...], step[...]
    v1 = v + 0.5 * dt * (a + a1) + dt * dt / 12.0 * (k - k1)
    x1 = x + 0.5 * dt * (v + v1) + dt * dt / 12.0 * (a - a1)
    new_pos[...] = jnp.where(on, x1, x)
    new_vel[...] = jnp.where(on, v1, v)
    new_acc[...] = jnp.where(on, a1, a)
    new_jerk[...] = jnp.where(on, k1, k)


def params(collective_id=None, limit=32 * 2**20):
    if collective_id is None:
        return pltpu.CompilerParams(vmem_limit_bytes=limit)
    return pltpu.CompilerParams(collective_id=collective_id, has_side_effects=True, vmem_limit_bytes=limit)


def per_device(positions, velocities, accels, jerks, masses, elapsed, active, live_tiles):
    rows = lax.axis_size("row")
    cols = lax.axis_size("col")
    width = positions.shape[1]
    blocks = 2 * rows
    plane, layers = cols // 2, rows // 2
    share = blocks // (2 * plane)
    total_stars = width * rows * cols
    dma, told = pltpu.SemaphoreType.DMA, pltpu.SemaphoreType.REGULAR
    sum_scratch = [VMEM((2 * share, 4, LANES), F32)] * 2 + [VMEM((plane, 2 * share, 4, LANES), F32)]

    x_pred = positions + elapsed * (velocities + elapsed * (0.5 * accels + elapsed * jerks / 6.0))
    v_pred = velocities + elapsed * (accels + elapsed * jerks / 2.0)
    ids, states, j_side, j_mass = pl.pallas_call(
        functools.partial(gather_kernel, rows, cols, total_stars),
        out_shape=(
            jax.ShapeDtypeStruct((rows, 2, LANES), jnp.int32),
            jax.ShapeDtypeStruct((blocks, 4, LANES), F32),
            jax.ShapeDtypeStruct((PARTS * width, LANES), BF16),
            jax.ShapeDtypeStruct((32, PARTS * width), BF16),
        ),
        in_specs=[vmem()] * 4 + [smem()],
        out_specs=(vmem(),) * 4,
        scratch_shapes=[VMEM((PARTS, 2, LANES), jnp.int32), VMEM((PARTS, 8, width), F32), VMEM((blocks, 4, LANES), F32)]
        + sum_scratch
        + [VMEM((6 * PARTS * width // LANES, 3 * LANES), BF16)]
        + [dma((6,)), dma((4,)), dma, dma]
        + [dma((2 * layers,)) for _ in range(3)]
        + [told, told],
        compiler_params=params(0),
        name="gather_states",
    )(x_pred, v_pred, masses, active.reshape(active.shape[0] // TILE, TILE), live_tiles)

    pair_count = rows * LANES * PARTS * width
    partial = pl.pallas_call(
        functools.partial(sweep_kernel, rows, cols),
        out_shape=jax.ShapeDtypeStruct((blocks, 4, LANES), F32),
        in_specs=[smem()] + [vmem()] * 4,
        out_specs=vmem(),
        scratch_shapes=[VMEM((rows + 2, 8, LANES), F32)],
        compiler_params=params(),
        cost_estimate=pl.CostEstimate(flops=200 * pair_count, bytes_accessed=2**20, transcendentals=pair_count),
        name="pair_sums",
    )(ids, ids, states, j_side, j_mass)

    forces = pl.pallas_call(
        functools.partial(deliver_kernel, rows, cols),
        out_shape=jax.ShapeDtypeStruct((2, plane, rows, share, 4, LANES), F32),
        in_specs=[vmem()],
        out_specs=vmem(),
        scratch_shapes=sum_scratch + [VMEM((rows, share, 4, LANES), F32), dma((6,)), dma((6,)), dma((plane,)), told, told],
        compiler_params=params(1),
        name="deliver_forces",
    )(partial)

    return pl.pallas_call(
        functools.partial(finish_kernel, rows, cols),
        out_shape=tuple(jax.ShapeDtypeStruct((3, width), F32) for _ in range(4)),
        in_specs=[smem()] + [vmem()] * 6,
        out_specs=(vmem(),) * 4,
        scratch_shapes=[VMEM((20 * width // LANES, LANES), F32), VMEM((8, width), F32)],
        compiler_params=params(),
        name="finish_step",
    )(ids, forces, positions, velocities, accels, jerks, elapsed)


def solution(mesh):
    stars = P(None, ("row", "col"))
    in_specs = (stars,) * 6 + (P("row"), P("row"))
    return jax.shard_map(per_device, mesh=mesh, in_specs=in_specs, out_specs=(stars,) * 4, check_vma=False)
```
